256 devices in a mesh: gx: 2 (over y_hi), gy: 2 (over core), vert: 64 (over x, y_lo, z).
Axes of the slice: x: 4, y: 4 (y_hi: 2, y_lo: 2; y = y_hi * 2 + y_lo), z: 8, core: 2. Of those that a mesh axis runs over, the one named last changes fastest.
Arguments:
- distribution: float32 [8000, 64, 256], P('vert', 'gx', 'gy'), may hold values from 0 to 13, as said below
- collision_rate: float32 [64, 256], P('gx', 'gy'), may hold values from 0.05 to 0.9
Outputs:
- advanced: float32 [8000, 64, 256], P('vert', 'gx', 'gy')
The draws below stay inside these ranges and needn't reach their ends.
Inputs may be any that keep to these rules, and one draw needn't show every extreme that they name: `distribution`: Nonnegative, of the shape of a local equilibrium with cell-to-cell variation.
All inputs are finite; a program needn't handle non-finite values.
Results may differ from the reference program's by a relative error of at most 0.0003.
Values sent between devices are 32-bit elements; how exact they have to be, the bound alone decides.
No kernel may reach another device: no remote copies, remote signals or barrier semaphores. Data moves between devices by JAX's collectives and lax.ppermute only.
A program may use at most 64 MiB of HBM per device.

```python
import math
import jax
import jax.numpy as jnp
from jax import lax

VG = 20
NZ = 2
STEPS = 2
VEL = 8000
NX = 64
NY = 128


def draw_distribution(key, part):
    keys = jax.random.split(jax.random.fold_in(key, 7), 6)
    shape = (NX, NY * NZ)
    density = jnp.exp(jax.random.uniform(keys[0], shape, jnp.float32, jnp.log(0.5), jnp.log(2.0)))
    flow_x = jax.random.uniform(keys[1], shape, jnp.float32, -0.6, 0.6)
    flow_y = jax.random.uniform(keys[2], shape, jnp.float32, -0.6, 0.6)
    flow_z = jax.random.uniform(keys[3], shape, jnp.float32, -0.6, 0.6)
    temper = jax.random.uniform(keys[4], shape, jnp.float32, 0.6, 1.5)
    noise = jax.random.uniform(keys[5], (VEL, NX, NY * NZ), jnp.float32, -0.4, 0.4)
    labels = jnp.arange(VEL, dtype=jnp.int32)

    def speed(index):
        return (4.5 * (2.0 * (index.astype(jnp.float32) + 0.5) / VG - 1.0))[:, None, None]
    diff_x = speed(labels // (VG * VG)) - flow_x[None]
    diff_y = speed(labels // VG % VG) - flow_y[None]
    diff_z = speed(labels % VG) - flow_z[None]
    amplitude = density / (temper * jnp.sqrt(temper))
    shape_part = jnp.exp(-(diff_x * diff_x + diff_y * diff_y + diff_z * diff_z) / (2.0 * temper[None]))
    return amplitude[None] * shape_part * (1.0 + noise)


def steps_of(stream_key, extent, pieces, smallest, high):
    def one(axis_at, shards_of):
        heights = jax.random.uniform(jax.random.fold_in(jax.random.fold_in(stream_key, 6), axis_at), (shards_of,), jnp.float32, smallest / len(pieces), high / len(pieces))
        return jnp.repeat(jnp.exp(heights), extent[axis_at] // shards_of).reshape((-1,) + (1,) * (len(extent) - axis_at - 1))

    factor_of = one(*pieces[0])
    for cut in pieces[1:]:
        factor_of = factor_of * one(*cut)
    return factor_of


def setup_inputs(seed: int = 0) -> dict:
    key_list = jax.random.split(jax.random.key(seed), 3)
    return {
        "distribution": draw_distribution(jax.random.fold_in(key_list[2], 71), 0),
        "collision_rate": jnp.clip(jnp.exp(math.log(0.9) - 2.8903717 * jax.random.uniform(key_list[1], (NX, NY * NZ), jnp.float32) ** steps_of(key_list[1], (NX, NY * NZ), ((0, 2), (1, 2)), -0.2, 0.2)), 0.05, 0.9),
    }


speed_max = 4.5
time_step = 0.3 / 4.5

def grid_speed(index):
    return speed_max * (2.0 * (index.astype(jnp.float32) + 0.5) / VG - 1.0)

def velocity_tables(first, count):
    labels = first + jnp.arange(count, dtype=jnp.int32)
    speed_x = grid_speed(labels // (VG * VG))
    speed_y = grid_speed(labels // VG % VG)
    speed_z = grid_speed(labels % VG)
    weight = (2.0 * speed_max / VG) ** 3 / (2.0 * math.pi) ** 1.5
    table = jnp.stack([weight * jnp.ones_like(speed_x), weight * speed_x, weight * speed_y, weight * speed_z, weight * (speed_x * speed_x + speed_y * speed_y + speed_z * speed_z)])
    return (speed_x, speed_y, speed_z, table)

def running(center, xpad, ypad, speed_x, speed_y, speed_z):
    shaped = (-1, 1, 1, 1)
    speed_x = speed_x.reshape(shaped)
    speed_y = speed_y.reshape(shaped)
    speed_z = speed_z.reshape(shaped)
    back_x = (3.0 * center - 4.0 * xpad[:, 1:-3] + xpad[:, :-4]) * 0.5
    ahead_x = (-3.0 * center + 4.0 * xpad[:, 3:-1] - xpad[:, 4:]) * 0.5
    back_y = (3.0 * center - 4.0 * ypad[:, :, 1:-3] + ypad[:, :, :-4]) * 0.5
    ahead_y = (-3.0 * center + 4.0 * ypad[:, :, 3:-1] - ypad[:, :, 4:]) * 0.5
    back_z = (3.0 * center - 4.0 * jnp.roll(center, 1, 3) + jnp.roll(center, 2, 3)) * 0.5
    ahead_z = (-3.0 * center + 4.0 * jnp.roll(center, -1, 3) - jnp.roll(center, -2, 3)) * 0.5
    flux = jnp.maximum(speed_x, 0.0) * back_x + jnp.minimum(speed_x, 0.0) * ahead_x
    flux = flux + jnp.maximum(speed_y, 0.0) * back_y + jnp.minimum(speed_y, 0.0) * ahead_y
    flux = flux + jnp.maximum(speed_z, 0.0) * back_z + jnp.minimum(speed_z, 0.0) * ahead_z
    return center - time_step * flux

def parameters(moments):
    density = moments[0]
    flow_x = moments[1] / density
    flow_y = moments[2] / density
    flow_z = moments[3] / density
    temper = (moments[4] / density - (flow_x * flow_x + flow_y * flow_y + flow_z * flow_z)) / 3.0
    return jnp.stack([density / (temper * jnp.sqrt(temper)), flow_x, flow_y, flow_z, 0.5 / temper])

def relax(moved, speed_x, speed_y, speed_z, params, rate):
    diff_x = speed_x[:, None] - params[1][None]
    diff_y = speed_y[:, None] - params[2][None]
    diff_z = speed_z[:, None] - params[3][None]
    maxwell = params[0][None] * jnp.exp(-params[4][None] * (diff_x * diff_x + diff_y * diff_y + diff_z * diff_z))
    return moved + rate[None] * (maxwell - moved)

def reference(distribution, collision_rate):
    rate = collision_rate.reshape(-1)
    firsts = jnp.arange(VG, dtype=jnp.int32) * (VG * VG)
    state = distribution
    for step in range(STEPS):
        blocks = state.reshape(VG, VG * VG, NX, NY, NZ)

        def sweep(carry, item):
            block, first = item
            speed_x, speed_y, speed_z, table = velocity_tables(first, VG * VG)
            xpad = jnp.pad(block, ((0, 0), (2, 2), (0, 0), (0, 0)), mode='wrap')
            ypad = jnp.pad(block, ((0, 0), (0, 0), (2, 2), (0, 0)), mode='wrap')
            moved = running(block, xpad, ypad, speed_x, speed_y, speed_z).reshape(VG * VG, -1)
            carry = carry + jnp.dot(table, moved, precision=lax.Precision.HIGHEST)
            return (carry, moved)
        moments, moved_all = lax.scan(sweep, jnp.zeros((5, NX * NY * NZ), jnp.float32), (blocks, firsts))
        params = parameters(moments)

        def collide(item):
            moved, first = item
            speed_x, speed_y, speed_z, table = velocity_tables(first, VG * VG)
            return relax(moved, speed_x, speed_y, speed_z, params, rate)
        state = lax.map(collide, (moved_all, firsts)).reshape(VEL, NX, NY * NZ)
    return state
```

```python
import math

import jax
import jax.numpy as jnp
from jax import lax
from jax.sharding import PartitionSpec as P

VG = 20
NZ = 2
STEPS = 2


speed_max = 4.5
time_step = 0.3 / 4.5


def with_halo(cells, sides, width):
    for axis, dim in sides:
        count = lax.axis_size(axis)
        head = lax.slice_in_dim(cells, 0, width, axis=dim)
        tail = lax.slice_in_dim(cells, cells.shape[dim] - width, cells.shape[dim], axis=dim)
        cells = jnp.concatenate(
            [
                lax.ppermute(tail, axis, [(i, (i + 1) % count) for i in range(count)]),
                cells,
                lax.ppermute(head, axis, [((i + 1) % count, i) for i in range(count)]),
            ],
            axis=dim,
        )
    return cells


def grid_speed(index):
    return speed_max * (2.0 * (index.astype(jnp.float32) + 0.5) / VG - 1.0)


def velocity_tables(first, count):
    labels = first + jnp.arange(count, dtype=jnp.int32)
    speed_x = grid_speed(labels // (VG * VG))
    speed_y = grid_speed(labels // VG % VG)
    speed_z = grid_speed(labels % VG)
    weight = (2.0 * speed_max / VG) ** 3 / (2.0 * math.pi) ** 1.5
    table = jnp.stack(
        [
            weight * jnp.ones_like(speed_x),
            weight * speed_x,
            weight * speed_y,
            weight * speed_z,
            weight * (speed_x * speed_x + speed_y * speed_y + speed_z * speed_z),
        ]
    )
    return (speed_x, speed_y, speed_z, table)


def running(center, xpad, ypad, speed_x, speed_y, speed_z):
    cols = center.shape[2]
    shaped = (-1, 1, 1)
    speed_x = speed_x.reshape(shaped)
    speed_y = speed_y.reshape(shaped)
    speed_z = speed_z.reshape(shaped)
    plane = lax.broadcasted_iota(jnp.int32, (1, 1, cols), 2) % NZ

    def below(offset):
        return jnp.where(
            plane >= offset, jnp.roll(center, offset, 2), jnp.roll(center, offset - NZ, 2)
        )

    def above(offset):
        return jnp.where(
            plane < NZ - offset, jnp.roll(center, -offset, 2), jnp.roll(center, NZ - offset, 2)
        )

    back_x = (3.0 * center - 4.0 * xpad[:, 1:-3] + xpad[:, :-4]) * 0.5
    ahead_x = (-3.0 * center + 4.0 * xpad[:, 3:-1] - xpad[:, 4:]) * 0.5
    back_y = (3.0 * center - 4.0 * ypad[:, :, NZ : NZ + cols] + ypad[:, :, :cols]) * 0.5
    ahead_y = (
        -3.0 * center
        + 4.0 * ypad[:, :, 3 * NZ : 3 * NZ + cols]
        - ypad[:, :, 4 * NZ : 4 * NZ + cols]
    ) * 0.5
    back_z = (3.0 * center - 4.0 * below(1) + below(2)) * 0.5
    ahead_z = (-3.0 * center + 4.0 * above(1) - above(2)) * 0.5
    flux = jnp.maximum(speed_x, 0.0) * back_x + jnp.minimum(speed_x, 0.0) * ahead_x
    flux = flux + jnp.maximum(speed_y, 0.0) * back_y + jnp.minimum(speed_y, 0.0) * ahead_y
    flux = flux + jnp.maximum(speed_z, 0.0) * back_z + jnp.minimum(speed_z, 0.0) * ahead_z
    return center - time_step * flux


def parameters(moments):
    density = moments[0]
    flow_x = moments[1] / density
    flow_y = moments[2] / density
    flow_z = moments[3] / density
    temper = (moments[4] / density - (flow_x * flow_x + flow_y * flow_y + flow_z * flow_z)) / 3.0
    return jnp.stack([density / (temper * jnp.sqrt(temper)), flow_x, flow_y, flow_z, 0.5 / temper])


def relax(moved, speed_x, speed_y, speed_z, params, rate):
    diff_x = speed_x[:, None] - params[1][None]
    diff_y = speed_y[:, None] - params[2][None]
    diff_z = speed_z[:, None] - params[3][None]
    maxwell = params[0][None] * jnp.exp(
        -params[4][None] * (diff_x * diff_x + diff_y * diff_y + diff_z * diff_z)
    )
    return moved + rate[None] * (maxwell - moved)


def sum_over_vert(partial):
    count = lax.axis_size("vert")
    rows, cells = partial.shape
    share = cells // count
    parts = jnp.transpose(partial.reshape(rows, count, share), (1, 0, 2)).reshape(count, -1)
    total = jnp.sum(lax.all_to_all(parts, "vert", 0, 0), axis=0)
    spread = lax.all_to_all(jnp.broadcast_to(total[None], parts.shape), "vert", 0, 0)
    return jnp.transpose(spread.reshape(count, rows, share), (1, 0, 2)).reshape(rows, cells)


def body(distribution, collision_rate):
    vel_local, rows_x, cols_yz = distribution.shape
    first = lax.axis_index("vert") * vel_local
    speed_x, speed_y, speed_z, table = velocity_tables(first, vel_local)
    rate = collision_rate.reshape(-1)
    state = distribution
    for step in range(STEPS):
        xpad = with_halo(state, (("gx", 1),), 2)
        ypad = with_halo(state, (("gy", 2),), 2 * NZ)
        moved = running(state, xpad, ypad, speed_x, speed_y, speed_z)
        moved = moved.reshape(vel_local, -1)
        partial_sum = jnp.dot(table, moved, precision=lax.Precision.HIGHEST)
        params = parameters(sum_over_vert(partial_sum))
        state = relax(moved, speed_x, speed_y, speed_z, params, rate).reshape(
            vel_local, rows_x, cols_yz
        )
    return state


def solution(mesh):
    placed = (P("vert", "gx", "gy"), P("gx", "gy"))
    return jax.shard_map(
        body, mesh=mesh, in_specs=placed, out_specs=P("vert", "gx", "gy"), check_vma=False
    )
```

```python
import math

import jax
import jax.numpy as jnp
from jax import lax
from jax.experimental import pallas as pl
from jax.experimental.pallas import tpu as pltpu
from jax.sharding import Mesh
from jax.sharding import PartitionSpec as P

VG = 20
VEL_LOCAL = 125
CHUNK = 5
CHUNKS = VEL_LOCAL // CHUNK
GROUPS = 7
ROWS = 32
LANES = 128

SPACING = 9.0 / VG
LOWEST = 4.5 * (1.0 / VG - 1.0)
DT = 0.3 / 4.5
WEIGHT = (9.0 / VG) ** 3 / (2.0 * math.pi) ** 1.5
SPEEDS = [LOWEST + SPACING * n for n in range(VG)]

VERT = ("x", "yl", "z")
PLANE = ("x", "yl")

ROW_SECOND = 5 * ROWS
ROW_SPILL_Y = 10 * ROWS
ROW_SPILL_X = 11 * ROWS
ROW_EDGE = 12 * ROWS
ROW_COUNT = 16 * ROWS

STACK = 72
NEAR_Y = 32
NEAR_X = 64


def speed_of(index):
    return index.astype(jnp.float32) * SPACING + LOWEST


def lane_index():
    return lax.broadcasted_iota(jnp.int32, (ROWS, LANES), 1)


def other_plane(tile, even):
    return jnp.where(even, pltpu.roll(tile, LANES - 1, 1), pltpu.roll(tile, 1, 1))


def chunk_place(first, chunk):
    slot = lax.rem(first, VG) + chunk * CHUNK
    group = lax.div(slot, VG)
    whole = lax.div(first, VG) + group
    index_x = lax.div(whole, VG)
    return group, index_x, whole - index_x * VG, slot - group * VG


def y_sides(lane, positive):
    shift = jnp.where(positive, 2, LANES - 2)
    one = ((lane + jnp.where(positive, 2, 0)) & (LANES - 1)) < 2
    two = ((lane + jnp.where(positive, 4, 0)) & (LANES - 1)) < 4
    return shift, one, two


def y_part(center, near, sides):
    shift, one, two = sides
    far = pltpu.roll(jnp.where(two, near, center), shift, 1)
    return pltpu.roll(jnp.where(one, near, center) - 0.25 * far, shift, 1)


def upwind(center, back, x_one, x_two, even, coef_x, coef_y, coef_z):
    return (
        center * (1.0 - 1.5 * (coef_x + coef_y) - 2.0 * coef_z)
        + (2.0 * coef_x) * (x_one - 0.25 * x_two)
        + (2.0 * coef_y) * back
        + (2.0 * coef_z) * other_plane(center, even)
    )


def first_kernel(place, f, f_near, f_edge, rate, kept, sums, groups, buf):
    device = place[0]
    first = device * VEL_LOCAL
    sign = jnp.where(device >= 32, 1, -1)
    lane = lane_index()
    even = lax.rem(lane, 2) == 0
    keep = 1.0 - rate[...]
    groups[...] = jnp.zeros_like(groups)

    def chunk(c, carry):
        group, index_x, index_y, index_z = chunk_place(first, c)
        coef_x = DT * jnp.abs(speed_of(index_x))
        coef_y = DT * jnp.abs(speed_of(index_y))
        positive = index_y >= VG // 2
        sides = y_sides(lane, positive)
        side = jnp.where(index_z >= VG // 2, 1.0, -1.0)
        acc = [None] * 4
        for t in range(CHUNK):
            v = c * CHUNK + t
            center = f[v]
            halo = f_edge[v]
            buf[t, 8:40] = center
            buf[t, 6:8] = halo
            buf[t, 40:42] = halo
            x_one = buf[t, pl.ds(8 - sign, ROWS)]
            x_two = buf[t, pl.ds(8 - 2 * sign, ROWS)]
            speed_z = speed_of(index_z + t)
            back = y_part(center, f_near[v], sides)
            moved = upwind(
                center, back, x_one, x_two, even, coef_x, coef_y, DT * speed_z * side
            )
            kept[v] = keep * moved
            power = moved
            for k in range(4):
                acc[k] = power if acc[k] is None else acc[k] + power
                if k < 3:
                    power = power * speed_z
        for k in range(3):
            groups[group, k] += acc[k]
            groups[group, 3 + k] += side * acc[k + 1]
        return carry

    lax.fori_loop(0, CHUNKS, chunk, 0)
    sums[...] = jnp.zeros_like(sums)

    def spread(group, carry):
        whole = lax.div(first, VG) + group
        index_x = lax.div(whole, VG)
        index_y = whole - index_x * VG
        speed_x = speed_of(index_x)
        speed_y = speed_of(index_y)
        coef_x = DT * jnp.abs(speed_x)
        coef_y = DT * jnp.abs(speed_y)
        positive = index_y >= VG // 2
        sides = y_sides(lane, positive)
        zero_rows = jnp.zeros((2, LANES), jnp.float32)

        def put(row, parts):
            squares = speed_x * speed_x + speed_y * speed_y
            count = parts[0].shape[0]
            for m, value in enumerate(
                (
                    parts[0],
                    speed_x * parts[0],
                    speed_y * parts[0],
                    parts[1],
                    squares * parts[0] + parts[2],
                )
            ):
                at = row + m * (ROWS if count == ROWS else 4)
                sums[at : at + count] += value

        level = [WEIGHT * groups[group, k] for k in range(6)]
        put(0, level[:3])
        second, near_y, near_x = [], [], []
        for k in range(3):
            center = keep * level[k]
            absolute = keep * level[3 + k]
            buf[k, 8:40] = center
            buf[k, 6:8] = zero_rows
            buf[k, 40:42] = zero_rows
            x_one = buf[k, pl.ds(8 - sign, ROWS)]
            x_two = buf[k, pl.ds(8 - 2 * sign, ROWS)]
            second.append(
                center * (1.0 - 1.5 * (coef_x + coef_y))
                - (2.0 * DT) * (absolute - other_plane(absolute, even))
                + (2.0 * coef_x) * (x_one - 0.25 * x_two)
                + (2.0 * coef_y) * y_part(center, 0.0, sides)
            )
            near_y.append(coef_y * jnp.where(sides[2], center, 0.0))
            tail = coef_x * jnp.maximum(sign, 0).astype(jnp.float32)
            head = coef_x * jnp.maximum(-sign, 0).astype(jnp.float32)
            near_x.append(
                jnp.concatenate([tail * buf[k, 38:40], head * buf[k, 8:10]], axis=0)
            )
        put(ROW_SECOND, second)
        put(ROW_SPILL_X, near_x)
        squares = speed_x * speed_x + speed_y * speed_y
        packed = sums[ROW_SPILL_Y : ROW_SPILL_Y + ROWS]
        for m, value in enumerate(
            (
                near_y[0],
                speed_x * near_y[0],
                speed_y * near_y[0],
                near_y[1],
                squares * near_y[0] + near_y[2],
            )
        ):
            packed = packed + (pltpu.roll(value, 8 * m, 1) if m else value)
        sums[ROW_SPILL_Y : ROW_SPILL_Y + ROWS] = packed
        return carry

    lax.fori_loop(0, GROUPS, spread, 0)
    for m in range(5):
        sums[ROW_EDGE + 4 * m : ROW_EDGE + 4 * m + 2] = sums[ROWS * m + 30 : ROWS * m + 32]
        sums[ROW_EDGE + 4 * m + 2 : ROW_EDGE + 4 * m + 4] = sums[ROWS * m : ROWS * m + 2]


def parameters(moments):
    density = moments[0]
    share = 1.0 / density
    flow_x = moments[1] * share
    flow_y = moments[2] * share
    flow_z = moments[3] * share
    temper = (moments[4] * share - (flow_x * flow_x + flow_y * flow_y + flow_z * flow_z)) / 3.0
    return density / (temper * jnp.sqrt(temper)), flow_x, flow_y, flow_z, 0.5 / temper


def products(part_x, part_y, part_z):
    yz = part_y[0] * part_z[0]
    return (
        part_x[0] * yz,
        part_x[1] * yz,
        part_x[0] * (part_y[1] * part_z[0]),
        part_x[0] * (part_y[0] * part_z[1]),
        part_x[2] * yz + part_x[0] * (part_y[2] * part_z[0] + part_y[0] * part_z[2]),
    )


def second_kernel(
    place, kept, kept_near, kept_edge, total, total_near, total_edge, rate, rate_near, rate_edge,
    out, first_mom, stack_rate, tables, kinds, table_two, base, buf,
):
    device = place[0]
    first = device * VEL_LOCAL
    sign = jnp.where(device >= 32, 1, -1)
    lane = lane_index()
    even = lax.rem(lane, 2) == 0
    rising = (2, lane >= LANES - 2, lane >= LANES - 4)
    falling = (LANES - 2, lane < 2, lane < 4)

    for m in range(5):
        first_mom[m, 0:32] = total[ROWS * m : ROWS * (m + 1)]
        first_mom[m, 32:64] = total_near[ROWS * m : ROWS * (m + 1)]
        first_mom[m, 64:72] = total[ROWS * m : ROWS * m + 8]
        first_mom[m, 64:68] = total_edge[ROWS + 4 * m : ROWS + 4 * m + 4]
    stack_rate[0:32] = rate[...]
    stack_rate[32:64] = rate_near[...]
    stack_rate[64:72] = rate[0:8]
    stack_rate[64:68] = rate_edge[...]

    def block(b, carry):
        at = pl.ds(pl.multiple_of(b * 8, 8), 8)
        amp, flow_x, flow_y, flow_z, inv = parameters([first_mom[m, at] for m in range(5)])
        scale = amp * stack_rate[at]
        base[at] = scale
        full, plus, minus = [], [], []
        for d, flow in enumerate((flow_x, flow_y, flow_z)):
            halves = []
            for half in range(2):
                level = [None] * 4
                for n in range(half * 10, half * 10 + 10):
                    gap = SPEEDS[n] - flow
                    value = jnp.exp(-(inv * gap * gap))
                    tables[d, n, at] = value
                    for k in range(4):
                        term = value if k == 0 else value * (SPEEDS[n] ** k)
                        level[k] = term if level[k] is None else level[k] + term
                halves.append(level)
            full.append([halves[0][k] + halves[1][k] for k in range(3)])
            plus.append([halves[1][k + 1] for k in range(3)])
            minus.append([-halves[0][k + 1] for k in range(3)])
        scale = scale * WEIGHT
        x, y, z = ([scale * part for part in full[0]]), full[1], full[2]
        sets = [
            products([scale * part for part in plus[0]], y, z),
            products([scale * part for part in minus[0]], y, z),
            products(x, plus[1], z),
            products(x, minus[1], z),
            products(x, y, [plus[2][k] + minus[2][k] for k in range(3)]),
        ]
        whole = products(x, y, z)
        for m in range(5):
            for s in range(5):
                kinds[s, m, at] = sets[s][m]
            kinds[5, m, at] = (
                whole[m]
                - (1.5 * DT) * ((sets[0][m] + sets[1][m]) + (sets[2][m] + sets[3][m]))
                - (2.0 * DT) * sets[4][m]
            )
        return carry

    lax.fori_loop(0, STACK // 8, block, 0)

    spill_y = total_near[ROW_SPILL_Y : ROW_SPILL_Y + ROWS]
    moments = []
    for m in range(5):
        own = slice(0, ROWS)
        near = slice(NEAR_Y, NEAR_Y + ROWS)
        result = total[ROW_SECOND + ROWS * m : ROW_SECOND + ROWS * (m + 1)] + kinds[5, m, own]
        result = result + (2.0 * DT) * other_plane(kinds[4, m, own], even)
        buf[0, 8:40] = kinds[0, m, own]
        buf[0, 6:8] = kinds[0, m, NEAR_X : NEAR_X + 2] + (1.0 / DT) * total_edge[4 * m : 4 * m + 2]
        result = result + (2.0 * DT) * (buf[0, 7:39] - 0.25 * buf[0, 6:38])
        buf[1, 8:40] = kinds[1, m, own]
        buf[1, 40:42] = (
            kinds[1, m, NEAR_X + 2 : NEAR_X + 4] + (1.0 / DT) * total_edge[4 * m + 2 : 4 * m + 4]
        )
        result = result + (2.0 * DT) * (buf[1, 9:41] - 0.25 * buf[1, 10:42])
        spill = pltpu.roll(spill_y, LANES - 8 * m, 1) if m else spill_y
        spill = (1.0 / DT) * spill
        result = result + (2.0 * DT) * y_part(kinds[2, m, own], kinds[2, m, near] + spill, rising)
        back = y_part(kinds[3, m, own], kinds[3, m, near] + spill, falling)
        moments.append(result + (2.0 * DT) * back)

    amp, flow_x, flow_y, flow_z, inv = parameters(moments)
    scale_two = amp * rate[...]
    keep = 1.0 - rate[...]
    for n in range(VG):
        gap = SPEEDS[n] - flow_z
        table_two[n] = jnp.exp(-(inv * gap * gap))
    table_two[VG] = scale_two
    table_two[VG + 1] = flow_x
    table_two[VG + 2] = flow_y
    table_two[VG + 3] = inv
    edge_at = NEAR_X + jnp.where(sign > 0, 0, 2)

    def chunk(c, carry):
        group, index_x, index_y, index_z = chunk_place(first, c)
        speed_x = speed_of(index_x)
        speed_y = speed_of(index_y)
        coef_x = DT * jnp.abs(speed_x)
        coef_y = DT * jnp.abs(speed_y)
        positive = index_y >= VG // 2
        sides = y_sides(lane, positive)
        side = jnp.where(index_z >= VG // 2, 1.0, -1.0)
        front = base[...] * tables[0, index_x] * tables[1, index_y]
        front_edge = (
            base[pl.ds(edge_at, 2)]
            * tables[0, index_x, pl.ds(edge_at, 2)]
            * tables[1, index_y, pl.ds(edge_at, 2)]
        )
        gap_x = speed_x - table_two[VG + 1]
        gap_y = speed_y - table_two[VG + 2]
        front_two = table_two[VG] * jnp.exp(
            -(table_two[VG + 3] * (gap_x * gap_x + gap_y * gap_y))
        )
        for t in range(CHUNK):
            v = c * CHUNK + t
            speed_z = speed_of(index_z + t)
            center = kept[v] + front[0:32] * tables[2, index_z + t, 0:32]
            near = kept_near[v] + front[32:64] * tables[2, index_z + t, 32:64]
            halo = kept_edge[v] + front_edge * tables[2, index_z + t, pl.ds(edge_at, 2)]
            buf[t, 8:40] = center
            buf[t, 6:8] = halo
            buf[t, 40:42] = halo
            x_one = buf[t, pl.ds(8 - sign, ROWS)]
            x_two = buf[t, pl.ds(8 - 2 * sign, ROWS)]
            moved = upwind(
                center, y_part(center, near, sides), x_one, x_two, even, coef_x, coef_y,
                DT * speed_z * side,
            )
            out[v] = keep * moved + front_two * table_two[index_z + t]
        return carry

    lax.fori_loop(0, CHUNKS, chunk, 0)


def vmem():
    return pl.BlockSpec(memory_space=pltpu.VMEM)


def smem():
    return pl.BlockSpec(memory_space=pltpu.SMEM)


SWAP = [(0, 1), (1, 0)]


def sum_over_vert(partial):
    parts = partial.reshape(8, 8, 8, LANES)
    share = jnp.sum(lax.all_to_all(parts, PLANE, 0, 0), axis=0)
    share = jnp.sum(lax.all_to_all(jnp.broadcast_to(share[None], parts.shape), "z", 0, 0), axis=0)
    whole = lax.all_to_all(jnp.broadcast_to(share[None], parts.shape), PLANE, 0, 0)
    return whole.reshape(ROW_COUNT, LANES)


def edge_rows(cells, forward):
    start = jnp.where(forward, ROWS - 2, 0)
    return lax.dynamic_slice_in_dim(cells, start, 2, axis=1)


def body(distribution, collision_rate):
    device = lax.axis_index(VERT)
    place = device.astype(jnp.int32).reshape(1)
    forward = device >= 32
    tile = jax.ShapeDtypeStruct((VEL_LOCAL, ROWS, LANES), jnp.float32)
    f_edge = lax.ppermute(edge_rows(distribution, forward), "gx", SWAP)
    f_near = lax.ppermute(distribution, "gy", SWAP)
    rate_near = lax.ppermute(collision_rate, "gy", SWAP)
    rate_edge = lax.ppermute(
        jnp.concatenate([collision_rate[ROWS - 2 :], collision_rate[:2]], axis=0), "gx", SWAP
    )
    kept, partial = pl.pallas_call(
        first_kernel,
        out_shape=(tile, jax.ShapeDtypeStruct((ROW_COUNT, LANES), jnp.float32)),
        in_specs=[smem(), vmem(), vmem(), vmem(), vmem()],
        out_specs=(vmem(), vmem()),
        scratch_shapes=[
            pltpu.VMEM((GROUPS, 6, ROWS, LANES), jnp.float32),
            pltpu.VMEM((CHUNK, 48, LANES), jnp.float32),
        ],
        compiler_params=pltpu.CompilerParams(vmem_limit_bytes=24 * 2**20),
        name="move_and_sum",
    )(place, distribution, f_near, f_edge, collision_rate)
    kept_edge = lax.ppermute(edge_rows(kept, forward), "gx", SWAP)
    kept_near = lax.ppermute(kept, "gy", SWAP)
    total = sum_over_vert(partial)
    total_near = lax.ppermute(total, "gy", SWAP)
    total_edge = lax.ppermute(total[ROW_SPILL_X : ROW_EDGE + ROWS], "gx", SWAP)
    return pl.pallas_call(
        second_kernel,
        out_shape=tile,
        in_specs=[smem()] + [vmem()] * 9,
        out_specs=vmem(),
        scratch_shapes=[
            pltpu.VMEM((5, STACK, LANES), jnp.float32),
            pltpu.VMEM((STACK, LANES), jnp.float32),
            pltpu.VMEM((3, VG, STACK, LANES), jnp.float32),
            pltpu.VMEM((6, 5, STACK, LANES), jnp.float32),
            pltpu.VMEM((VG + 4, ROWS, LANES), jnp.float32),
            pltpu.VMEM((STACK, LANES), jnp.float32),
            pltpu.VMEM((CHUNK, 48, LANES), jnp.float32),
        ],
        compiler_params=pltpu.CompilerParams(vmem_limit_bytes=32 * 2**20),
        name="collide_move_collide",
    )(
        place, kept, kept_near, kept_edge, total, total_near, total_edge,
        collision_rate, rate_near, rate_edge,
    )


def solution(mesh):
    split = Mesh(mesh.devices.reshape(2, 2, 4, 2, 8), ("gx", "gy", "x", "yl", "z"))
    placed = (P(VERT, "gx", "gy"), P("gx", "gy"))
    return jax.shard_map(
        body, mesh=split, in_specs=placed, out_specs=P(VERT, "gx", "gy"), check_vma=False
    )
```

```python
import functools
import math

import jax
import jax.numpy as jnp
from jax import lax
from jax.experimental import pallas as pl
from jax.experimental.pallas import tpu as pltpu
from jax.sharding import Mesh
from jax.sharding import PartitionSpec as P

VG = 20
VEL_LOCAL = 125
CHUNK = 5
CHUNKS = VEL_LOCAL // CHUNK
STEPS = 5
STEP_CHUNKS = CHUNKS // STEPS
PIECE = VEL_LOCAL // STEPS
GROUPS = 7
ROWS = 32
LANES = 128

SPACING = 9.0 / VG
LOWEST = 4.5 * (1.0 / VG - 1.0)
DT = 0.3 / 4.5
WEIGHT = (9.0 / VG) ** 3 / (2.0 * math.pi) ** 1.5
SPEEDS = [LOWEST + SPACING * n for n in range(VG)]

VERT = ("x", "yl", "z")
PLANE = ("x", "yl")

ROW_SECOND = 5 * ROWS
ROW_SPILL_Y = 10 * ROWS
ROW_SPILL_X = 11 * ROWS
ROW_EDGE = 12 * ROWS
ROW_RATE = 13 * ROWS
ROW_COUNT = 14 * ROWS


def speed_of(index):
    return index.astype(jnp.float32) * SPACING + LOWEST


def lane_index():
    return lax.broadcasted_iota(jnp.int32, (ROWS, LANES), 1)


def other_plane(tile, even):
    return jnp.where(even, pltpu.roll(tile, LANES - 1, 1), pltpu.roll(tile, 1, 1))


def chunk_place(first, chunk):
    slot = lax.rem(first, VG) + chunk * CHUNK
    group = lax.div(slot, VG)
    whole = lax.div(first, VG) + group
    index_x = lax.div(whole, VG)
    return group, index_x, whole - index_x * VG, slot - group * VG


def y_part(center, near, sides):
    shift, one, two = sides
    far = pltpu.roll(jnp.where(two, near, center), shift, 1)
    return pltpu.roll(jnp.where(one, near, center) - 0.25 * far, shift, 1)


def upwind(center, back, x_one, x_two, even, coef_x, coef_y, coef_z):
    return (
        center * (1.0 - 1.5 * (coef_x + coef_y) - 2.0 * coef_z)
        + (2.0 * coef_x) * (x_one - 0.25 * x_two)
        + (2.0 * coef_y) * back
        + (2.0 * coef_z) * other_plane(center, even)
    )


def static_sides(positive):
    lane = lane_index()
    if positive:
        return 2, lane >= LANES - 2, lane >= LANES - 4
    return LANES - 2, lane < 2, lane < 4


def each_sign(positive, run):
    for value in (True, False):
        pl.when(positive if value else jnp.logical_not(positive))(functools.partial(run, value))


def x_steps(buf, slot, center, halo, forward):
    buf[slot, 8:40] = center
    if forward:
        buf[slot, 6:8] = halo
        return buf[slot, 7:39], buf[slot, 6:38]
    buf[slot, 40:42] = halo
    return buf[slot, 9:41], buf[slot, 10:42]


def load_piece(f, held, sem, piece):
    rows = pl.ds(piece * PIECE, PIECE)
    return pltpu.make_async_copy(f.at[rows], held.at[rows], sem.at[piece])


def send_kernel(place, f, out, band, sem):
    def take(forward):
        copy = pltpu.make_async_copy(f.at[:, pl.ds(24 if forward else 0, 8)], band, sem)
        copy.start()
        copy.wait()
        out[...] = band[:, 6:8] if forward else band[:, 0:2]

    each_sign(place[0] >= 32, take)


def inside_kernel(
    place, f, f_near, rate, kept, kept_edge, groups, held, held_near, held_rate, buf, sem, sem_near,
    sem_rate,
):
    rate_copy = pltpu.make_async_copy(rate, held_rate, sem_rate)
    rate_copy.start()
    for piece in range(STEPS):
        load_piece(f, held, sem, piece).start()
        load_piece(f_near, held_near, sem_near, piece).start()
    rate_copy.wait()
    device = place[0]
    first = device * VEL_LOCAL
    even = lax.rem(lane_index(), 2) == 0
    keep = 1.0 - held_rate[...]
    groups[...] = jnp.zeros_like(groups)

    def move(forward):
        def chunk(c, carry):
            group, index_x, index_y, index_z = chunk_place(first, c)
            coef_x = DT * jnp.abs(speed_of(index_x))
            coef_y = DT * jnp.abs(speed_of(index_y))
            side = jnp.where(index_z >= VG // 2, 1.0, -1.0)

            def run(rising):
                sides = static_sides(rising)
                acc = [None] * 4
                for t in range(CHUNK):
                    v = c * CHUNK + t
                    center = held[v]
                    x_one, x_two = x_steps(
                        buf, t, center, jnp.zeros((2, LANES), jnp.float32), forward
                    )
                    speed_z = speed_of(index_z + t)
                    back = y_part(center, held_near[v], sides)
                    moved = upwind(
                        center, back, x_one, x_two, even, coef_x, coef_y, DT * speed_z * side
                    )
                    left = keep * moved
                    kept[v] = left
                    kept_edge[v] = left[30:32] if forward else left[0:2]
                    power = moved
                    for k in range(4):
                        acc[k] = power if acc[k] is None else acc[k] + power
                        if k < 3:
                            power = power * speed_z
                for k in range(3):
                    groups[group, k] += acc[k]
                    groups[group, 3 + k] += side * acc[k + 1]

            each_sign(index_y >= VG // 2, run)
            return carry

        def piece(p, carry):
            load_piece(f, held, sem, p).wait()
            load_piece(f_near, held_near, sem_near, p).wait()
            return lax.fori_loop(p * STEP_CHUNKS, (p + 1) * STEP_CHUNKS, chunk, carry)

        lax.fori_loop(0, STEPS, piece, 0)

    each_sign(device >= 32, move)


def edge_kernel(
    place, kept_in, groups_in, f_edge, rate, kept, sums, groups, edge, buf, sem
):
    del kept_in
    device = place[0]
    first = device * VEL_LOCAL
    groups[...] = groups_in[...]
    even = lax.rem(lane_index(), 2) == 0
    keep = 1.0 - rate[...]

    def enter(forward):
        rows = slice(0, 2) if forward else slice(30, 32)
        inner = slice(0, 2) if forward else slice(6, 8)
        none = jnp.zeros((1, LANES), jnp.float32)
        band = kept.at[:, pl.ds(0 if forward else 24, 8)]
        load = pltpu.make_async_copy(band, edge, sem)
        load.start()
        load.wait()

        def chunk(c, carry):
            group, index_x, _, index_z = chunk_place(first, c)
            coef = (2.0 * DT) * jnp.abs(speed_of(index_x))
            side = jnp.where(index_z >= VG // 2, 1.0, -1.0)
            acc = [None] * 4
            for t in range(CHUNK):
                v = c * CHUNK + t
                halo = f_edge[v]
                one = [halo[1:2], none] if forward else [none, halo[0:1]]
                power = coef * (jnp.concatenate(one, axis=0) - 0.25 * halo)
                edge[v, inner] += keep[rows] * power
                speed_z = speed_of(index_z + t)
                for k in range(4):
                    acc[k] = power if acc[k] is None else acc[k] + power
                    if k < 3:
                        power = power * speed_z
            for k in range(3):
                groups[group, k, rows] += acc[k]
                groups[group, 3 + k, rows] += side * acc[k + 1]
            return carry

        lax.fori_loop(0, CHUNKS, chunk, 0)
        store = pltpu.make_async_copy(edge, band, sem)
        store.start()
        return store

    def spread(forward):
        def one(group, carry):
            whole = lax.div(first, VG) + group
            index_x = lax.div(whole, VG)
            index_y = whole - index_x * VG
            speed_x = speed_of(index_x)
            speed_y = speed_of(index_y)
            coef_x = DT * jnp.abs(speed_x)
            coef_y = DT * jnp.abs(speed_y)
            squares = speed_x * speed_x + speed_y * speed_y

            def five(parts):
                return (
                    parts[0],
                    speed_x * parts[0],
                    speed_y * parts[0],
                    parts[1],
                    squares * parts[0] + parts[2],
                )

            def run(rising):
                sides = static_sides(rising)
                level = [WEIGHT * groups[group, k] for k in range(6)]
                for m, value in enumerate(five(level)):
                    sums[ROWS * m : ROWS * (m + 1)] += value
                second, near_y, near_x = [], [], []
                for k in range(3):
                    center = keep * level[k]
                    absolute = keep * level[3 + k]
                    x_one, x_two = x_steps(
                        buf, k, center, jnp.zeros((2, LANES), jnp.float32), forward
                    )
                    second.append(
                        center * (1.0 - 1.5 * (coef_x + coef_y))
                        - (2.0 * DT) * (absolute - other_plane(absolute, even))
                        + (2.0 * coef_x) * (x_one - 0.25 * x_two)
                        + (2.0 * coef_y) * y_part(center, 0.0, sides)
                    )
                    near_y.append(coef_y * jnp.where(sides[2], center, 0.0))
                    near_x.append(coef_x * (center[30:32] if forward else center[0:2]))
                for m, value in enumerate(five(second)):
                    sums[ROW_SECOND + ROWS * m : ROW_SECOND + ROWS * (m + 1)] += value
                for m, value in enumerate(five(near_x)):
                    at = ROW_SPILL_X + 4 * m + (0 if forward else 2)
                    sums[at : at + 2] += value
                packed = sums[ROW_SPILL_Y : ROW_SPILL_Y + ROWS]
                for m, value in enumerate(five(near_y)):
                    packed = packed + (pltpu.roll(value, 8 * m, 1) if m else value)
                sums[ROW_SPILL_Y : ROW_SPILL_Y + ROWS] = packed

            each_sign(index_y >= VG // 2, run)
            return carry

        lax.fori_loop(0, GROUPS, one, 0)

    sums[...] = jnp.zeros_like(sums)

    def both(forward):
        store = enter(forward)
        spread(forward)
        store.wait()

    each_sign(device >= 32, both)
    for m in range(5):
        at = ROW_EDGE + 4 * m
        sums[at : at + 2] = sums[ROWS * m + 30 : ROWS * m + 32]
        sums[at + 2 : at + 4] = sums[ROWS * m : ROWS * m + 2]

    @pl.when(device == 0)
    def _():
        at = ROW_EDGE + 20
        sums[at : at + 2] = rate[30:32]
        sums[at + 2 : at + 4] = rate[0:2]
        sums[ROW_RATE : ROW_RATE + ROWS] = rate[...]


def parameters(moments):
    density = moments[0]
    share = 1.0 / density
    flow_x = moments[1] * share
    flow_y = moments[2] * share
    flow_z = moments[3] * share
    temper = (moments[4] * share - (flow_x * flow_x + flow_y * flow_y + flow_z * flow_z)) / 3.0
    return density / (temper * jnp.sqrt(temper)), flow_x, flow_y, flow_z, 0.5 / temper


def products(part_x, part_y, part_z):
    yz = part_y[0] * part_z[0]
    return (
        part_x[0] * yz,
        part_x[1] * yz,
        part_x[0] * (part_y[1] * part_z[0]),
        part_x[0] * (part_y[0] * part_z[1]),
        part_x[2] * yz + part_x[0] * (part_y[2] * part_z[0] + part_y[0] * part_z[2]),
    )


def one_block(at, moments, rate, base, tables, kinds, wanted):
    amp, flow_x, flow_y, flow_z, inv = parameters(moments)
    scale = amp * rate
    base[at] = scale
    full, plus, minus = [], [], []
    for d, flow in enumerate((flow_x, flow_y, flow_z)):
        halves = []
        for half in range(2):
            level = [None] * 4
            for n in range(half * 10, half * 10 + 10):
                gap = SPEEDS[n] - flow
                value = jnp.exp(-(inv * gap * gap))
                tables[d, n, at] = value
                for k in range(4):
                    term = value if k == 0 else value * (SPEEDS[n] ** k)
                    level[k] = term if level[k] is None else level[k] + term
            halves.append(level)
        full.append([halves[0][k] + halves[1][k] for k in range(3)])
        plus.append([halves[1][k + 1] for k in range(3)])
        minus.append([-halves[0][k + 1] for k in range(3)])
    scale = scale * WEIGHT
    x, y, z = [scale * part for part in full[0]], full[1], full[2]
    sets = {}
    if "x" in wanted:
        sets[0] = products([scale * part for part in plus[0]], y, z)
        sets[1] = products([scale * part for part in minus[0]], y, z)
    if "y" in wanted:
        sets[2] = products(x, plus[1], z)
        sets[3] = products(x, minus[1], z)
    if "z" in wanted:
        sets[4] = products(x, y, [plus[2][k] + minus[2][k] for k in range(3)])
        whole = products(x, y, z)
        sets[5] = [
            whole[m]
            - (1.5 * DT) * ((sets[0][m] + sets[1][m]) + (sets[2][m] + sets[3][m]))
            - (2.0 * DT) * sets[4][m]
            for m in range(5)
        ]
    for s, values in sets.items():
        for m in range(5):
            kinds[s, m, at] = values[m]


def table_kernel(wanted, total, rate, base, tables, kinds):
    def block(b, carry):
        def rows(start):
            return pl.ds(pl.multiple_of(start + b * 8, 8), 8)

        one_block(
            rows(0), [total[rows(ROWS * m)] for m in range(5)], rate[rows(0)], base, tables, kinds,
            wanted,
        )
        return carry

    lax.fori_loop(0, ROWS // 8, block, 0)


def second_kernel(
    place, kept, kept_near, kept_edge, total, total_near, total_edge, rate,
    base, tables, kinds, base_near, tables_near, kinds_near,
    out, base_edge, tables_edge, kinds_edge, table_two, done, buf, sem,
):
    device = place[0]
    first = device * VEL_LOCAL
    even = lax.rem(lane_index(), 2) == 0
    keep = 1.0 - rate[...]

    def edge(row):
        rows = total_edge[row : row + 4]
        return jnp.concatenate([rows, rows], axis=0)

    one_block(
        slice(0, 8), [edge(ROWS + 4 * m) for m in range(5)], edge(ROWS + 20), base_edge,
        tables_edge, kinds_edge, "x",
    )
    spill_y = total_near[ROW_SPILL_Y : ROW_SPILL_Y + ROWS]
    moments = []
    for m in range(5):
        result = total[ROW_SECOND + ROWS * m : ROW_SECOND + ROWS * (m + 1)] + kinds[5, m]
        x_one, x_two = x_steps(
            buf, 0, kinds[0, m],
            kinds_edge[0, m, 0:2] + (1.0 / DT) * total_edge[4 * m : 4 * m + 2], True,
        )
        x_low, x_lower = x_steps(
            buf, 1, kinds[1, m],
            kinds_edge[1, m, 2:4] + (1.0 / DT) * total_edge[4 * m + 2 : 4 * m + 4], False,
        )
        spill = pltpu.roll(spill_y, LANES - 8 * m, 1) if m else spill_y
        spill = (1.0 / DT) * spill
        moments.append(
            result
            + (2.0 * DT)
            * (
                other_plane(kinds[4, m], even)
                + (x_one - 0.25 * x_two)
                + (x_low - 0.25 * x_lower)
                + y_part(kinds[2, m], kinds_near[2, m] + spill, static_sides(True))
                + y_part(kinds[3, m], kinds_near[3, m] + spill, static_sides(False))
            )
        )
    amp, flow_x, flow_y, flow_z, inv = parameters(moments)
    for n in range(VG):
        gap = SPEEDS[n] - flow_z
        table_two[n] = jnp.exp(-(inv * gap * gap))
    table_two[VG] = amp * rate[...]
    table_two[VG + 1] = flow_x
    table_two[VG + 2] = flow_y
    table_two[VG + 3] = inv


    def move(forward):
        row = 0 if forward else 2

        def chunk(c, carry):
            group, index_x, index_y, index_z = chunk_place(first, c)
            speed_x = speed_of(index_x)
            speed_y = speed_of(index_y)
            coef_x = DT * jnp.abs(speed_x)
            coef_y = DT * jnp.abs(speed_y)
            side = jnp.where(index_z >= VG // 2, 1.0, -1.0)

            def run(rising):
                sides = static_sides(rising)
                front = base[...] * tables[0, index_x] * tables[1, index_y]
                front_near = base_near[...] * tables_near[0, index_x] * tables_near[1, index_y]
                front_edge = base_edge[...] * tables_edge[0, index_x] * tables_edge[1, index_y]
                gap_x = speed_x - table_two[VG + 1]
                gap_y = speed_y - table_two[VG + 2]
                front_two = table_two[VG] * jnp.exp(
                    -(table_two[VG + 3] * (gap_x * gap_x + gap_y * gap_y))
                )
                for t in range(CHUNK):
                    v = c * CHUNK + t
                    n = index_z + t
                    center = kept[v] + front * tables[2, n]
                    near = kept_near[v] + front_near * tables_near[2, n]
                    halo = kept_edge[v] + (front_edge * tables_edge[2, n])[row : row + 2]
                    x_one, x_two = x_steps(buf, t, center, halo, forward)
                    moved = upwind(
                        center, y_part(center, near, sides), x_one, x_two, even, coef_x, coef_y,
                        DT * speed_of(n) * side,
                    )
                    done[v] = keep * moved + front_two * table_two[n]

            each_sign(index_y >= VG // 2, run)
            return carry

        def piece(p, carry):
            lax.fori_loop(p * STEP_CHUNKS, (p + 1) * STEP_CHUNKS, chunk, 0)
            load_piece(done, out, sem, p).start()
            return carry

        lax.fori_loop(0, STEPS, piece, 0)

    each_sign(device >= 32, move)
    for piece in range(STEPS):
        load_piece(done, out, sem, piece).wait()


def vmem():
    return pl.BlockSpec(memory_space=pltpu.VMEM)


def in_hbm(x):
    return pltpu.with_memory_space_constraint(x, pltpu.HBM)


def hbm():
    return pl.BlockSpec(memory_space=pltpu.HBM)


def anywhere():
    return pl.BlockSpec(memory_space=pl.ANY)


def smem():
    return pl.BlockSpec(memory_space=pltpu.SMEM)


SWAP = [(0, 1), (1, 0)]


def sum_over_vert(partial, beside):
    parts = partial.reshape(8, -1, 8, LANES)
    share = jnp.sum(lax.all_to_all(parts, PLANE, 0, 0), axis=0)
    share = jnp.sum(lax.all_to_all(jnp.broadcast_to(share[None], parts.shape), "z", 0, 0), axis=0)
    share, beside = lax.optimization_barrier((share, beside))
    whole = lax.all_to_all(jnp.broadcast_to(share[None], parts.shape), PLANE, 0, 0)
    return whole.reshape(ROW_COUNT, LANES), beside


def f32(*shape):
    return jax.ShapeDtypeStruct(shape, jnp.float32)


def tables_of(total, rate, wanted, name):
    return pl.pallas_call(
        functools.partial(table_kernel, wanted),
        out_shape=(
            f32(ROWS, LANES), f32(3, VG, ROWS, LANES), f32(6, 5, ROWS, LANES)
        ),
        in_specs=[vmem(), vmem()],
        out_specs=(vmem(), vmem(), vmem()),
        compiler_params=pltpu.CompilerParams(vmem_limit_bytes=16 * 2**20),
        cost_estimate=pl.CostEstimate(flops=8000000, bytes_accessed=3000000, transcendentals=250000),
        name=name,
    )(total, rate)


def body(distribution, collision_rate):
    device = lax.axis_index(VERT)
    place = device.astype(jnp.int32).reshape(1)
    f_edge = pl.pallas_call(
        send_kernel,
        out_shape=f32(VEL_LOCAL, 2, LANES),
        in_specs=[smem(), hbm()],
        out_specs=vmem(),
        scratch_shapes=[pltpu.VMEM((VEL_LOCAL, 8, LANES), jnp.float32), pltpu.SemaphoreType.DMA],
        compiler_params=pltpu.CompilerParams(vmem_limit_bytes=24 * 2**20),
        cost_estimate=pl.CostEstimate(flops=0, bytes_accessed=600000, transcendentals=0),
        name="send_rows",
    )(place, in_hbm(distribution))
    f_edge = lax.ppermute(f_edge, "gx", SWAP)
    f_near = lax.ppermute(distribution, "gy", SWAP)
    kept, kept_edge, groups = pl.pallas_call(
        inside_kernel,
        out_shape=(
            f32(VEL_LOCAL, ROWS, LANES), f32(VEL_LOCAL, 2, LANES), f32(GROUPS, 6, ROWS, LANES)
        ),
        in_specs=[smem(), hbm(), hbm(), hbm()],
        out_specs=(vmem(), vmem(), vmem()),
        scratch_shapes=[
            pltpu.VMEM((VEL_LOCAL, ROWS, LANES), jnp.float32),
            pltpu.VMEM((VEL_LOCAL, ROWS, LANES), jnp.float32),
            pltpu.VMEM((ROWS, LANES), jnp.float32),
            pltpu.VMEM((CHUNK, 48, LANES), jnp.float32),
            pltpu.SemaphoreType.DMA((STEPS,)),
            pltpu.SemaphoreType.DMA((STEPS,)),
            pltpu.SemaphoreType.DMA,
        ],
        compiler_params=pltpu.CompilerParams(vmem_limit_bytes=16 * 2**20),
        cost_estimate=pl.CostEstimate(flops=50000000, bytes_accessed=6000000, transcendentals=0),
        name="move_inside",
    )(place, in_hbm(distribution), in_hbm(f_near), in_hbm(collision_rate))
    kept_edge = lax.ppermute(kept_edge, "gx", SWAP)
    kept, partial = pl.pallas_call(
        edge_kernel,
        out_shape=(f32(VEL_LOCAL, ROWS, LANES), f32(ROW_COUNT, LANES)),
        in_specs=[smem(), anywhere()] + [vmem()] * 3,
        out_specs=(anywhere(), vmem()),
        scratch_shapes=[
            pltpu.VMEM((GROUPS, 6, ROWS, LANES), jnp.float32),
            pltpu.VMEM((VEL_LOCAL, 8, LANES), jnp.float32),
            pltpu.VMEM((CHUNK, 48, LANES), jnp.float32),
            pltpu.SemaphoreType.DMA,
        ],
        input_output_aliases={1: 0},
        compiler_params=pltpu.CompilerParams(vmem_limit_bytes=16 * 2**20),
        name="enter_and_sum",
    )(place, kept, groups, f_edge, collision_rate)
    kept_near = lax.ppermute(kept, "gy", SWAP)
    total, kept_edge = sum_over_vert(partial, kept_edge)
    total_near = lax.ppermute(total, "gy", SWAP)
    total_edge = lax.ppermute(total[ROW_SPILL_X : ROW_EDGE + ROWS], "gx", SWAP)
    own = tables_of(total, collision_rate, "xyz", "tables_own")
    near = tables_of(total_near, total_near[ROW_RATE : ROW_RATE + ROWS], "y", "tables_near")
    return pl.pallas_call(
        second_kernel,
        out_shape=f32(VEL_LOCAL, ROWS, LANES),
        in_specs=[smem()] + [vmem()] * 13,
        out_specs=anywhere(),
        scratch_shapes=[
            pltpu.VMEM((8, LANES), jnp.float32),
            pltpu.VMEM((3, VG, 8, LANES), jnp.float32),
            pltpu.VMEM((2, 5, 8, LANES), jnp.float32),
            pltpu.VMEM((VG + 4, ROWS, LANES), jnp.float32),
            pltpu.VMEM((VEL_LOCAL, ROWS, LANES), jnp.float32),
            pltpu.VMEM((CHUNK, 48, LANES), jnp.float32),
            pltpu.SemaphoreType.DMA((STEPS,)),
        ],
        compiler_params=pltpu.CompilerParams(vmem_limit_bytes=24 * 2**20),
        name="collide_move_collide",
    )(
        place, kept, kept_near, kept_edge, total, total_near, total_edge, collision_rate, *own,
        *near,
    )


def solution(mesh):
    split = Mesh(mesh.devices.reshape(2, 2, 4, 2, 8), ("gx", "gy", "x", "yl", "z"))
    placed = (P(VERT, "gx", "gy"), P("gx", "gy"))
    return jax.shard_map(
        body, mesh=split, in_specs=placed, out_specs=P(VERT, "gx", "gy"), check_vma=False
    )
```

```python
import functools
import math

import jax
import jax.numpy as jnp
from jax import lax
from jax.experimental import pallas as pl
from jax.experimental.pallas import tpu as pltpu
from jax.sharding import Mesh
from jax.sharding import PartitionSpec as P

VG = 20
VEL_LOCAL = 125
CHUNK = 5
CHUNKS = VEL_LOCAL // CHUNK
STEPS = 5
STEP_CHUNKS = CHUNKS // STEPS
PIECE = VEL_LOCAL // STEPS
GROUPS = 7
ROWS = 32
LANES = 128

SPACING = 9.0 / VG
LOWEST = 4.5 * (1.0 / VG - 1.0)
DT = 0.3 / 4.5
WEIGHT = (9.0 / VG) ** 3 / (2.0 * math.pi) ** 1.5
SPEEDS = [LOWEST + SPACING * n for n in range(VG)]

VERT = ("x", "yl", "z")
PLANE = ("x", "yl")

ROW_SECOND = 5 * ROWS
ROW_SPILL_Y = 10 * ROWS
ROW_SPILL_X = 11 * ROWS
ROW_EDGE = 12 * ROWS
ROW_RATE = 13 * ROWS
ROW_COUNT = 14 * ROWS


def speed_of(index):
    return index.astype(jnp.float32) * SPACING + LOWEST


def lane_index():
    return lax.broadcasted_iota(jnp.int32, (ROWS, LANES), 1)


def other_plane(tile, even):
    return jnp.where(even, pltpu.roll(tile, LANES - 1, 1), pltpu.roll(tile, 1, 1))


def chunk_place(first, chunk):
    slot = lax.rem(first, VG) + chunk * CHUNK
    group = lax.div(slot, VG)
    whole = lax.div(first, VG) + group
    index_x = lax.div(whole, VG)
    return group, index_x, whole - index_x * VG, slot - group * VG


def y_sides(positive):
    lane = lane_index()
    if positive is True:
        return 2, 4, lane >= LANES - 2, lane >= LANES - 4
    if positive is False:
        return LANES - 2, LANES - 4, lane < 2, lane < 4
    one = ((lane + jnp.where(positive, 2, 0)) & (LANES - 1)) < 2
    two = ((lane + jnp.where(positive, 4, 0)) & (LANES - 1)) < 4
    return jnp.where(positive, 2, LANES - 2), jnp.where(positive, 4, LANES - 4), one, two


def y_part(center, near, sides):
    shift_one, shift_two, one, two = sides
    return pltpu.roll(jnp.where(one, near, center), shift_one, 1) - 0.25 * pltpu.roll(
        jnp.where(two, near, center), shift_two, 1
    )


def upwind(center, back, x_one, x_two, even, coef_x, coef_y, coef_z):
    return (
        center * (1.0 - 1.5 * (coef_x + coef_y) - 2.0 * coef_z)
        + (2.0 * coef_x) * (x_one - 0.25 * x_two)
        + (2.0 * coef_y) * back
        + (2.0 * coef_z) * other_plane(center, even)
    )


def each_sign(positive, run):
    for value in (True, False):
        pl.when(positive if value else jnp.logical_not(positive))(functools.partial(run, value))


def x_steps(buf, slot, center, halo, forward):
    buf[slot, 8:40] = center
    if forward:
        buf[slot, 6:8] = halo
        return buf[slot, 7:39], buf[slot, 6:38]
    buf[slot, 40:42] = halo
    return buf[slot, 9:41], buf[slot, 10:42]


def load_piece(f, held, sem, piece):
    rows = pl.ds(piece * PIECE, PIECE)
    return pltpu.make_async_copy(f.at[rows], held.at[rows], sem.at[piece])


def send_kernel(place, f, out, band, sem):
    def take(forward):
        copy = pltpu.make_async_copy(f.at[:, pl.ds(24 if forward else 0, 8)], band, sem)
        copy.start()
        copy.wait()
        out[...] = band[:, 6:8] if forward else band[:, 0:2]

    each_sign(place[0] >= 32, take)


def inside_kernel(
    place, f, f_near, rate, kept, kept_edge, groups, held, held_near, held_rate, buf, sem, sem_near,
    sem_rate,
):
    rate_copy = pltpu.make_async_copy(rate, held_rate, sem_rate)
    rate_copy.start()
    for piece in range(STEPS):
        load_piece(f, held, sem, piece).start()
        load_piece(f_near, held_near, sem_near, piece).start()
    rate_copy.wait()
    device = place[0]
    first = device * VEL_LOCAL
    even = lax.rem(lane_index(), 2) == 0
    keep = 1.0 - held_rate[...]
    groups[...] = jnp.zeros_like(groups)

    def move(forward):
        def chunk(c, carry):
            group, index_x, index_y, index_z = chunk_place(first, c)
            coef_x = DT * jnp.abs(speed_of(index_x))
            coef_y = DT * jnp.abs(speed_of(index_y))
            side = jnp.where(index_z >= VG // 2, 1.0, -1.0)

            sides = y_sides(index_y >= VG // 2)
            acc = [None] * 4
            for t in range(CHUNK):
                v = c * CHUNK + t
                center = held[v]
                x_one, x_two = x_steps(
                    buf, t, center, jnp.zeros((2, LANES), jnp.float32), forward
                )
                speed_z = speed_of(index_z + t)
                back = y_part(center, held_near[v], sides)
                moved = upwind(
                    center, back, x_one, x_two, even, coef_x, coef_y, DT * speed_z * side
                )
                left = keep * moved
                kept[v] = left
                kept_edge[v] = left[30:32] if forward else left[0:2]
                power = moved
                for k in range(4):
                    acc[k] = power if acc[k] is None else acc[k] + power
                    if k < 3:
                        power = power * speed_z
            for k in range(3):
                groups[group, k] += acc[k]
                groups[group, 3 + k] += side * acc[k + 1]

            return carry

        def piece(p, carry):
            load_piece(f, held, sem, p).wait()
            load_piece(f_near, held_near, sem_near, p).wait()
            return lax.fori_loop(p * STEP_CHUNKS, (p + 1) * STEP_CHUNKS, chunk, carry)

        lax.fori_loop(0, STEPS, piece, 0)

    each_sign(device >= 32, move)


def edge_kernel(
    place, kept_in, groups_in, f_edge, rate, kept, sums, groups, edge, buf, sem
):
    del kept_in
    device = place[0]
    first = device * VEL_LOCAL
    groups[...] = groups_in[...]
    even = lax.rem(lane_index(), 2) == 0
    keep = 1.0 - rate[...]

    def enter(forward):
        rows = slice(0, 2) if forward else slice(30, 32)
        inner = slice(0, 2) if forward else slice(6, 8)
        none = jnp.zeros((1, LANES), jnp.float32)
        band = kept.at[:, pl.ds(0 if forward else 24, 8)]
        load = pltpu.make_async_copy(band, edge, sem)
        load.start()
        load.wait()

        def chunk(c, carry):
            group, index_x, _, index_z = chunk_place(first, c)
            coef = (2.0 * DT) * jnp.abs(speed_of(index_x))
            side = jnp.where(index_z >= VG // 2, 1.0, -1.0)
            acc = [None] * 4
            for t in range(CHUNK):
                v = c * CHUNK + t
                halo = f_edge[v]
                one = [halo[1:2], none] if forward else [none, halo[0:1]]
                power = coef * (jnp.concatenate(one, axis=0) - 0.25 * halo)
                edge[v, inner] += keep[rows] * power
                speed_z = speed_of(index_z + t)
                for k in range(4):
                    acc[k] = power if acc[k] is None else acc[k] + power
                    if k < 3:
                        power = power * speed_z
            for k in range(3):
                groups[group, k, rows] += acc[k]
                groups[group, 3 + k, rows] += side * acc[k + 1]
            return carry

        lax.fori_loop(0, CHUNKS, chunk, 0)
        store = pltpu.make_async_copy(edge, band, sem)
        store.start()
        return store

    def spread(forward):
        def one(group, carry):
            whole = lax.div(first, VG) + group
            index_x = lax.div(whole, VG)
            index_y = whole - index_x * VG
            speed_x = speed_of(index_x)
            speed_y = speed_of(index_y)
            coef_x = DT * jnp.abs(speed_x)
            coef_y = DT * jnp.abs(speed_y)
            squares = speed_x * speed_x + speed_y * speed_y

            def five(parts):
                return (
                    parts[0],
                    speed_x * parts[0],
                    speed_y * parts[0],
                    parts[1],
                    squares * parts[0] + parts[2],
                )

            sides = y_sides(index_y >= VG // 2)
            level = [WEIGHT * groups[group, k] for k in range(6)]
            for m, value in enumerate(five(level)):
                sums[ROWS * m : ROWS * (m + 1)] += value
            second, near_y, near_x = [], [], []
            for k in range(3):
                center = keep * level[k]
                absolute = keep * level[3 + k]
                x_one, x_two = x_steps(
                    buf, k, center, jnp.zeros((2, LANES), jnp.float32), forward
                )
                second.append(
                    center * (1.0 - 1.5 * (coef_x + coef_y))
                    - (2.0 * DT) * (absolute - other_plane(absolute, even))
                    + (2.0 * coef_x) * (x_one - 0.25 * x_two)
                    + (2.0 * coef_y) * y_part(center, 0.0, sides)
                )
                near_y.append(coef_y * jnp.where(sides[3], center, 0.0))
                near_x.append(coef_x * (center[30:32] if forward else center[0:2]))
            for m, value in enumerate(five(second)):
                sums[ROW_SECOND + ROWS * m : ROW_SECOND + ROWS * (m + 1)] += value
            for m, value in enumerate(five(near_x)):
                at = ROW_SPILL_X + 4 * m + (0 if forward else 2)
                sums[at : at + 2] += value
            packed = sums[ROW_SPILL_Y : ROW_SPILL_Y + ROWS]
            for m, value in enumerate(five(near_y)):
                packed = packed + (pltpu.roll(value, 8 * m, 1) if m else value)
            sums[ROW_SPILL_Y : ROW_SPILL_Y + ROWS] = packed

            return carry

        lax.fori_loop(0, GROUPS, one, 0)

    sums[...] = jnp.zeros_like(sums)

    def both(forward):
        store = enter(forward)
        spread(forward)
        store.wait()

    each_sign(device >= 32, both)
    for m in range(5):
        at = ROW_EDGE + 4 * m
        sums[at : at + 2] = sums[ROWS * m + 30 : ROWS * m + 32]
        sums[at + 2 : at + 4] = sums[ROWS * m : ROWS * m + 2]

    @pl.when(device == 0)
    def _():
        at = ROW_EDGE + 20
        sums[at : at + 2] = rate[30:32]
        sums[at + 2 : at + 4] = rate[0:2]
        sums[ROW_RATE : ROW_RATE + ROWS] = rate[...]


def parameters(moments):
    density = moments[0]
    share = 1.0 / density
    flow_x = moments[1] * share
    flow_y = moments[2] * share
    flow_z = moments[3] * share
    temper = (moments[4] * share - (flow_x * flow_x + flow_y * flow_y + flow_z * flow_z)) / 3.0
    return density / (temper * jnp.sqrt(temper)), flow_x, flow_y, flow_z, 0.5 / temper


def products(part_x, part_y, part_z):
    yz = part_y[0] * part_z[0]
    return (
        part_x[0] * yz,
        part_x[1] * yz,
        part_x[0] * (part_y[1] * part_z[0]),
        part_x[0] * (part_y[0] * part_z[1]),
        part_x[2] * yz + part_x[0] * (part_y[2] * part_z[0] + part_y[0] * part_z[2]),
    )


def one_block(at, moments, rate, base, tables, kinds, wanted):
    amp, flow_x, flow_y, flow_z, inv = parameters(moments)
    scale = amp * rate
    base[at] = scale
    full, plus, minus = [], [], []
    for d, flow in enumerate((flow_x, flow_y, flow_z)):
        halves = []
        for half in range(2):
            level = [None] * 4
            for n in range(half * 10, half * 10 + 10):
                gap = SPEEDS[n] - flow
                value = jnp.exp(-(inv * gap * gap))
                tables[d, n, at] = value
                for k in range(4):
                    term = value if k == 0 else value * (SPEEDS[n] ** k)
                    level[k] = term if level[k] is None else level[k] + term
            halves.append(level)
        full.append([halves[0][k] + halves[1][k] for k in range(3)])
        plus.append([halves[1][k + 1] for k in range(3)])
        minus.append([-halves[0][k + 1] for k in range(3)])
    scale = scale * WEIGHT
    x, y, z = [scale * part for part in full[0]], full[1], full[2]
    sets = {}
    if "x" in wanted:
        sets[0] = products([scale * part for part in plus[0]], y, z)
        sets[1] = products([scale * part for part in minus[0]], y, z)
    if "y" in wanted:
        sets[2] = products(x, plus[1], z)
        sets[3] = products(x, minus[1], z)
    if "z" in wanted:
        sets[4] = products(x, y, [plus[2][k] + minus[2][k] for k in range(3)])
        whole = products(x, y, z)
        sets[5] = [
            whole[m]
            - (1.5 * DT) * ((sets[0][m] + sets[1][m]) + (sets[2][m] + sets[3][m]))
            - (2.0 * DT) * sets[4][m]
            for m in range(5)
        ]
    for s, values in sets.items():
        for m in range(5):
            kinds[s, m, at] = values[m]


def table_kernel(wanted, total, rate, base, tables, kinds):
    def block(b, carry):
        def rows(start):
            return pl.ds(pl.multiple_of(start + b * 8, 8), 8)

        one_block(
            rows(0), [total[rows(ROWS * m)] for m in range(5)], rate[rows(0)], base, tables, kinds,
            wanted,
        )
        return carry

    lax.fori_loop(0, ROWS // 8, block, 0)


def second_inside_kernel(
    place, kept, kept_near, rate, base, tables, base_near, tables_near, moved_part, buf
):
    device = place[0]
    first = device * VEL_LOCAL
    even = lax.rem(lane_index(), 2) == 0

    def move(forward):
        def chunk(c, carry):
            group, index_x, index_y, index_z = chunk_place(first, c)
            coef_x = DT * jnp.abs(speed_of(index_x))
            coef_y = DT * jnp.abs(speed_of(index_y))
            side = jnp.where(index_z >= VG // 2, 1.0, -1.0)
            sides = y_sides(index_y >= VG // 2)
            front = base[...] * tables[0, index_x] * tables[1, index_y]
            front_near = base_near[...] * tables_near[0, index_x] * tables_near[1, index_y]
            for t in range(CHUNK):
                v = c * CHUNK + t
                n = index_z + t
                center = kept[v] + front * tables[2, n]
                near = kept_near[v] + front_near * tables_near[2, n]
                x_one, x_two = x_steps(
                    buf, t, center, jnp.zeros((2, LANES), jnp.float32), forward
                )
                moved_part[v] = upwind(
                    center, y_part(center, near, sides), x_one, x_two, even, coef_x, coef_y,
                    DT * speed_of(n) * side,
                )
            return carry

        lax.fori_loop(0, CHUNKS, chunk, 0)

    each_sign(device >= 32, move)


def second_kernel(
    place, moved_part, kept_edge, total, total_near, total_edge, rate, kinds, kinds_near,
    out, base_edge, tables_edge, kinds_edge, table_two, done, buf, sem,
):
    device = place[0]
    first = device * VEL_LOCAL
    even = lax.rem(lane_index(), 2) == 0
    keep = 1.0 - rate[...]

    def edge(row):
        rows = total_edge[row : row + 4]
        return jnp.concatenate([rows, rows], axis=0)

    one_block(
        slice(0, 8), [edge(ROWS + 4 * m) for m in range(5)], edge(ROWS + 20), base_edge,
        tables_edge, kinds_edge, "x",
    )
    spill_y = total_near[ROW_SPILL_Y : ROW_SPILL_Y + ROWS]
    moments = []
    for m in range(5):
        result = total[ROW_SECOND + ROWS * m : ROW_SECOND + ROWS * (m + 1)] + kinds[5, m]
        x_one, x_two = x_steps(
            buf, 0, kinds[0, m],
            kinds_edge[0, m, 0:2] + (1.0 / DT) * total_edge[4 * m : 4 * m + 2], True,
        )
        x_low, x_lower = x_steps(
            buf, 1, kinds[1, m],
            kinds_edge[1, m, 2:4] + (1.0 / DT) * total_edge[4 * m + 2 : 4 * m + 4], False,
        )
        spill = pltpu.roll(spill_y, LANES - 8 * m, 1) if m else spill_y
        spill = (1.0 / DT) * spill
        moments.append(
            result
            + (2.0 * DT)
            * (
                other_plane(kinds[4, m], even)
                + (x_one - 0.25 * x_two)
                + (x_low - 0.25 * x_lower)
                + y_part(kinds[2, m], kinds_near[2, m] + spill, y_sides(True))
                + y_part(kinds[3, m], kinds_near[3, m] + spill, y_sides(False))
            )
        )
    amp, flow_x, flow_y, flow_z, inv = parameters(moments)
    for n in range(VG):
        gap = SPEEDS[n] - flow_z
        table_two[n] = jnp.exp(-(inv * gap * gap))
    table_two[VG] = amp * rate[...]
    table_two[VG + 1] = flow_x
    table_two[VG + 2] = flow_y
    table_two[VG + 3] = inv


    def move(forward):
        row = 0 if forward else 2
        rows = slice(0, 2) if forward else slice(30, 32)
        none = jnp.zeros((1, LANES), jnp.float32)

        def chunk(c, carry):
            group, index_x, index_y, index_z = chunk_place(first, c)
            speed_x = speed_of(index_x)
            coef = (2.0 * DT) * jnp.abs(speed_x)
            gap_x = speed_x - table_two[VG + 1]
            gap_y = speed_of(index_y) - table_two[VG + 2]
            front_two = table_two[VG] * jnp.exp(
                -(table_two[VG + 3] * (gap_x * gap_x + gap_y * gap_y))
            )
            front_edge = base_edge[...] * tables_edge[0, index_x] * tables_edge[1, index_y]
            for t in range(CHUNK):
                v = c * CHUNK + t
                n = index_z + t
                halo = kept_edge[v] + (front_edge * tables_edge[2, n])[row : row + 2]
                one = [halo[1:2], none] if forward else [none, halo[0:1]]
                entered = coef * (jnp.concatenate(one, axis=0) - 0.25 * halo)
                done[v] = keep * moved_part[v] + front_two * table_two[n]
                done[v, rows] += keep[rows] * entered
            return carry

        def piece(p, carry):
            lax.fori_loop(p * STEP_CHUNKS, (p + 1) * STEP_CHUNKS, chunk, 0)
            load_piece(done, out, sem, p).start()
            return carry

        lax.fori_loop(0, STEPS, piece, 0)

    each_sign(device >= 32, move)
    for piece in range(STEPS):
        load_piece(done, out, sem, piece).wait()


def vmem():
    return pl.BlockSpec(memory_space=pltpu.VMEM)


def in_hbm(x):
    return pltpu.with_memory_space_constraint(x, pltpu.HBM)


def hbm():
    return pl.BlockSpec(memory_space=pltpu.HBM)


def anywhere():
    return pl.BlockSpec(memory_space=pl.ANY)


def smem():
    return pl.BlockSpec(memory_space=pltpu.SMEM)


SWAP = [(0, 1), (1, 0)]


def sum_over_vert(partial, beside):
    parts = partial.reshape(8, -1, 8, LANES)
    share = jnp.sum(lax.all_to_all(parts, PLANE, 0, 0), axis=0)
    share = jnp.sum(lax.all_to_all(jnp.broadcast_to(share[None], parts.shape), "z", 0, 0), axis=0)
    share, beside = lax.optimization_barrier((share, beside))
    whole = lax.all_to_all(jnp.broadcast_to(share[None], parts.shape), PLANE, 0, 0)
    return whole.reshape(ROW_COUNT, LANES), beside


def f32(*shape):
    return jax.ShapeDtypeStruct(shape, jnp.float32)


def tables_of(total, rate, wanted, name):
    return pl.pallas_call(
        functools.partial(table_kernel, wanted),
        out_shape=(
            f32(ROWS, LANES), f32(3, VG, ROWS, LANES), f32(6, 5, ROWS, LANES)
        ),
        in_specs=[vmem(), vmem()],
        out_specs=(vmem(), vmem(), vmem()),
        compiler_params=pltpu.CompilerParams(vmem_limit_bytes=16 * 2**20),
        cost_estimate=pl.CostEstimate(flops=8000000, bytes_accessed=3000000, transcendentals=250000),
        name=name,
    )(total, rate)


def body(distribution, collision_rate):
    device = lax.axis_index(VERT)
    place = device.astype(jnp.int32).reshape(1)
    f_edge = pl.pallas_call(
        send_kernel,
        out_shape=f32(VEL_LOCAL, 2, LANES),
        in_specs=[smem(), hbm()],
        out_specs=vmem(),
        scratch_shapes=[pltpu.VMEM((VEL_LOCAL, 8, LANES), jnp.float32), pltpu.SemaphoreType.DMA],
        compiler_params=pltpu.CompilerParams(vmem_limit_bytes=24 * 2**20),
        cost_estimate=pl.CostEstimate(flops=0, bytes_accessed=600000, transcendentals=0),
        name="send_rows",
    )(place, in_hbm(distribution))
    f_edge = lax.ppermute(f_edge, "gx", SWAP)
    f_near = lax.ppermute(distribution, "gy", SWAP)
    kept, kept_edge, groups = pl.pallas_call(
        inside_kernel,
        out_shape=(
            f32(VEL_LOCAL, ROWS, LANES), f32(VEL_LOCAL, 2, LANES), f32(GROUPS, 6, ROWS, LANES)
        ),
        in_specs=[smem(), hbm(), hbm(), hbm()],
        out_specs=(vmem(), vmem(), vmem()),
        scratch_shapes=[
            pltpu.VMEM((VEL_LOCAL, ROWS, LANES), jnp.float32),
            pltpu.VMEM((VEL_LOCAL, ROWS, LANES), jnp.float32),
            pltpu.VMEM((ROWS, LANES), jnp.float32),
            pltpu.VMEM((CHUNK, 48, LANES), jnp.float32),
            pltpu.SemaphoreType.DMA((STEPS,)),
            pltpu.SemaphoreType.DMA((STEPS,)),
            pltpu.SemaphoreType.DMA,
        ],
        compiler_params=pltpu.CompilerParams(vmem_limit_bytes=16 * 2**20),
        cost_estimate=pl.CostEstimate(flops=50000000, bytes_accessed=6000000, transcendentals=0),
        name="move_inside",
    )(place, in_hbm(distribution), in_hbm(f_near), in_hbm(collision_rate))
    kept_edge = lax.ppermute(kept_edge, "gx", SWAP)
    kept, partial = pl.pallas_call(
        edge_kernel,
        out_shape=(f32(VEL_LOCAL, ROWS, LANES), f32(ROW_COUNT, LANES)),
        in_specs=[smem(), anywhere()] + [vmem()] * 3,
        out_specs=(anywhere(), vmem()),
        scratch_shapes=[
            pltpu.VMEM((GROUPS, 6, ROWS, LANES), jnp.float32),
            pltpu.VMEM((VEL_LOCAL, 8, LANES), jnp.float32),
            pltpu.VMEM((CHUNK, 48, LANES), jnp.float32),
            pltpu.SemaphoreType.DMA,
        ],
        input_output_aliases={1: 0},
        compiler_params=pltpu.CompilerParams(vmem_limit_bytes=16 * 2**20),
        name="enter_and_sum",
    )(place, kept, groups, f_edge, collision_rate)
    kept_near = lax.ppermute(kept, "gy", SWAP)
    total, kept_edge = sum_over_vert(partial, kept_edge)
    total_near = lax.ppermute(total, "gy", SWAP)
    total_edge = lax.ppermute(total[ROW_SPILL_X : ROW_EDGE + ROWS], "gx", SWAP)
    own = tables_of(total, collision_rate, "xyz", "tables_own")
    near = tables_of(total_near, total_near[ROW_RATE : ROW_RATE + ROWS], "y", "tables_near")
    moved_part = pl.pallas_call(
        second_inside_kernel,
        out_shape=f32(VEL_LOCAL, ROWS, LANES),
        in_specs=[smem()] + [vmem()] * 7,
        out_specs=vmem(),
        scratch_shapes=[pltpu.VMEM((CHUNK, 48, LANES), jnp.float32)],
        compiler_params=pltpu.CompilerParams(vmem_limit_bytes=16 * 2**20),
        cost_estimate=pl.CostEstimate(flops=50000000, bytes_accessed=6000000, transcendentals=0),
        name="move_inside_two",
    )(place, kept, kept_near, collision_rate, *own[:2], *near[:2])
    return pl.pallas_call(
        second_kernel,
        out_shape=f32(VEL_LOCAL, ROWS, LANES),
        in_specs=[smem()] + [vmem()] * 8,
        out_specs=anywhere(),
        scratch_shapes=[
            pltpu.VMEM((8, LANES), jnp.float32),
            pltpu.VMEM((3, VG, 8, LANES), jnp.float32),
            pltpu.VMEM((2, 5, 8, LANES), jnp.float32),
            pltpu.VMEM((VG + 4, ROWS, LANES), jnp.float32),
            pltpu.VMEM((VEL_LOCAL, ROWS, LANES), jnp.float32),
            pltpu.VMEM((CHUNK, 48, LANES), jnp.float32),
            pltpu.SemaphoreType.DMA((STEPS,)),
        ],
        compiler_params=pltpu.CompilerParams(vmem_limit_bytes=24 * 2**20),
        name="collide_two",
    )(
        place, moved_part, kept_edge, total, total_near, total_edge, collision_rate, own[2],
        near[2],
    )


def solution(mesh):
    split = Mesh(mesh.devices.reshape(2, 2, 4, 2, 8), ("gx", "gy", "x", "yl", "z"))
    placed = (P(VERT, "gx", "gy"), P("gx", "gy"))
    return jax.shard_map(
        body, mesh=split, in_specs=placed, out_specs=P(VERT, "gx", "gy"), check_vma=False
    )
```

```python
import functools
import math

import jax
import jax.numpy as jnp
from jax import lax
from jax.experimental import pallas as pl
from jax.experimental.pallas import tpu as pltpu
from jax.sharding import Mesh
from jax.sharding import PartitionSpec as P

VG = 20
VEL_LOCAL = 125
CHUNK = 5
CHUNKS = VEL_LOCAL // CHUNK
STEPS = 5
STEP_CHUNKS = CHUNKS // STEPS
PIECE = VEL_LOCAL // STEPS
GROUPS = 7
ROWS = 32
LANES = 128

SPACING = 9.0 / VG
LOWEST = 4.5 * (1.0 / VG - 1.0)
DT = 0.3 / 4.5
WEIGHT = (9.0 / VG) ** 3 / (2.0 * math.pi) ** 1.5
SPEEDS = [LOWEST + SPACING * n for n in range(VG)]

VERT = ("x", "yl", "z")
PLANE = ("x", "yl")

ROW_SECOND = 5 * ROWS
ROW_SPILL_Y = 10 * ROWS
ROW_SPILL_X = 11 * ROWS
ROW_EDGE = 12 * ROWS
ROW_RATE = 13 * ROWS
ROW_COUNT = 14 * ROWS


def speed_of(index):
    return index.astype(jnp.float32) * SPACING + LOWEST


def lane_index():
    return lax.broadcasted_iota(jnp.int32, (ROWS, LANES), 1)


def other_plane(tile, even):
    return jnp.where(even, pltpu.roll(tile, LANES - 1, 1), pltpu.roll(tile, 1, 1))


def chunk_place(first, chunk):
    slot = lax.rem(first, VG) + chunk * CHUNK
    group = lax.div(slot, VG)
    whole = lax.div(first, VG) + group
    index_x = lax.div(whole, VG)
    return group, index_x, whole - index_x * VG, slot - group * VG


def y_sides(positive):
    lane = lane_index()
    if positive is True:
        return 2, 4, lane >= LANES - 2, lane >= LANES - 4
    if positive is False:
        return LANES - 2, LANES - 4, lane < 2, lane < 4
    one = ((lane + jnp.where(positive, 2, 0)) & (LANES - 1)) < 2
    two = ((lane + jnp.where(positive, 4, 0)) & (LANES - 1)) < 4
    return jnp.where(positive, 2, LANES - 2), jnp.where(positive, 4, LANES - 4), one, two


def y_part(center, near, sides):
    shift_one, shift_two, one, two = sides
    return pltpu.roll(jnp.where(one, near, center), shift_one, 1) - 0.25 * pltpu.roll(
        jnp.where(two, near, center), shift_two, 1
    )


def upwind(center, back, x_one, x_two, even, coef_x, coef_y, coef_z):
    return (
        center * (1.0 - 1.5 * (coef_x + coef_y) - 2.0 * coef_z)
        + (2.0 * coef_x) * (x_one - 0.25 * x_two)
        + (2.0 * coef_y) * back
        + (2.0 * coef_z) * other_plane(center, even)
    )


def each_sign(positive, run):
    for value in (True, False):
        pl.when(positive if value else jnp.logical_not(positive))(functools.partial(run, value))


def x_steps(buf, slot, center, halo, forward):
    buf[slot, 8:40] = center
    if forward:
        buf[slot, 6:8] = halo
        return buf[slot, 7:39], buf[slot, 6:38]
    buf[slot, 40:42] = halo
    return buf[slot, 9:41], buf[slot, 10:42]


def load_piece(f, held, sem, piece):
    rows = pl.ds(piece * PIECE, PIECE)
    return pltpu.make_async_copy(f.at[rows], held.at[rows], sem.at[piece])


def x_inside(center, forward):
    row = lax.broadcasted_iota(jnp.int32, (ROWS, LANES), 0)
    if forward:
        return [jnp.where(row >= n, pltpu.roll(center, n, 0), 0.0) for n in (1, 2)]
    return [jnp.where(row < ROWS - n, pltpu.roll(center, ROWS - n, 0), 0.0) for n in (1, 2)]


def send_kernel(place, f, out, band, sem):
    def take(forward):
        copy = pltpu.make_async_copy(f.at[:, pl.ds(24 if forward else 0, 8)], band, sem)
        copy.start()
        copy.wait()
        out[...] = band[:, 6:8] if forward else band[:, 0:2]

    each_sign(place[0] >= 32, take)


def inside_kernel(
    place, f, f_near, rate, kept, kept_edge, groups, held, held_near, held_rate, sem, sem_near,
    sem_rate,
):
    rate_copy = pltpu.make_async_copy(rate, held_rate, sem_rate)
    rate_copy.start()
    for piece in range(STEPS):
        load_piece(f, held, sem, piece).start()
        load_piece(f_near, held_near, sem_near, piece).start()
    rate_copy.wait()
    device = place[0]
    first = device * VEL_LOCAL
    even = lax.rem(lane_index(), 2) == 0
    keep = 1.0 - held_rate[...]
    groups[...] = jnp.zeros_like(groups)

    def move(forward):
        def chunk(c, carry):
            group, index_x, index_y, index_z = chunk_place(first, c)
            coef_x = DT * jnp.abs(speed_of(index_x))
            coef_y = DT * jnp.abs(speed_of(index_y))
            side = jnp.where(index_z >= VG // 2, 1.0, -1.0)

            sides = y_sides(index_y >= VG // 2)
            acc = [None] * 4
            at = [c * CHUNK + t for t in range(CHUNK)]
            speeds = [speed_of(index_z + t) for t in range(CHUNK)]
            centers = [held[v] for v in at]
            nears = [held_near[v] for v in at]
            backs = [y_part(center, near, sides) for center, near in zip(centers, nears)]
            moved = [
                upwind(center, back, *x_inside(center, forward), even, coef_x, coef_y,
                       DT * speed * side)
                for center, back, speed in zip(centers, backs, speeds)
            ]
            for value, speed in zip(moved, speeds):
                power = value
                for k in range(4):
                    acc[k] = power if acc[k] is None else acc[k] + power
                    if k < 3:
                        power = power * speed
            for v, value in zip(at, moved):
                left = keep * value
                kept[v] = left
                kept_edge[v] = left[30:32] if forward else left[0:2]
            for k in range(3):
                groups[group, k] += acc[k]
                groups[group, 3 + k] += side * acc[k + 1]

            return carry

        def piece(p, carry):
            load_piece(f, held, sem, p).wait()
            load_piece(f_near, held_near, sem_near, p).wait()
            for c in range(STEP_CHUNKS):
                chunk(p * STEP_CHUNKS + c, carry)
            return carry

        lax.fori_loop(0, STEPS, piece, 0)

    each_sign(device >= 32, move)


def edge_kernel(
    place, kept_in, groups_in, f_edge, rate, kept, sums, groups, edge, buf, sem
):
    del kept_in
    device = place[0]
    first = device * VEL_LOCAL
    groups[...] = groups_in[...]
    even = lax.rem(lane_index(), 2) == 0
    keep = 1.0 - rate[...]

    def enter(forward):
        rows = slice(0, 2) if forward else slice(30, 32)
        inner = slice(0, 2) if forward else slice(6, 8)
        none = jnp.zeros((1, LANES), jnp.float32)
        band = kept.at[:, pl.ds(0 if forward else 24, 8)]
        load = pltpu.make_async_copy(band, edge, sem)
        load.start()
        load.wait()

        def chunk(c, carry):
            group, index_x, _, index_z = chunk_place(first, c)
            coef = (2.0 * DT) * jnp.abs(speed_of(index_x))
            side = jnp.where(index_z >= VG // 2, 1.0, -1.0)
            acc = [None] * 4
            for t in range(CHUNK):
                v = c * CHUNK + t
                halo = f_edge[v]
                one = [halo[1:2], none] if forward else [none, halo[0:1]]
                power = coef * (jnp.concatenate(one, axis=0) - 0.25 * halo)
                edge[v, inner] += keep[rows] * power
                speed_z = speed_of(index_z + t)
                for k in range(4):
                    acc[k] = power if acc[k] is None else acc[k] + power
                    if k < 3:
                        power = power * speed_z
            for k in range(3):
                groups[group, k, rows] += acc[k]
                groups[group, 3 + k, rows] += side * acc[k + 1]
            return carry

        def some(p, carry):
            for c in range(STEP_CHUNKS):
                chunk(p * STEP_CHUNKS + c, carry)
            return carry

        lax.fori_loop(0, STEPS, some, 0)
        store = pltpu.make_async_copy(edge, band, sem)
        store.start()
        return store

    def spread(forward):
        def one(group, carry):
            whole = lax.div(first, VG) + group
            index_x = lax.div(whole, VG)
            index_y = whole - index_x * VG
            speed_x = speed_of(index_x)
            speed_y = speed_of(index_y)
            coef_x = DT * jnp.abs(speed_x)
            coef_y = DT * jnp.abs(speed_y)
            squares = speed_x * speed_x + speed_y * speed_y

            def five(parts):
                return (
                    parts[0],
                    speed_x * parts[0],
                    speed_y * parts[0],
                    parts[1],
                    squares * parts[0] + parts[2],
                )

            sides = y_sides(index_y >= VG // 2)
            level = [WEIGHT * groups[group, k] for k in range(6)]
            for m, value in enumerate(five(level)):
                sums[ROWS * m : ROWS * (m + 1)] += value
            second, near_y, near_x = [], [], []
            for k in range(3):
                center = keep * level[k]
                absolute = keep * level[3 + k]
                x_one, x_two = x_steps(
                    buf, k, center, jnp.zeros((2, LANES), jnp.float32), forward
                )
                second.append(
                    center * (1.0 - 1.5 * (coef_x + coef_y))
                    - (2.0 * DT) * (absolute - other_plane(absolute, even))
                    + (2.0 * coef_x) * (x_one - 0.25 * x_two)
                    + (2.0 * coef_y) * y_part(center, 0.0, sides)
                )
                near_y.append(coef_y * jnp.where(sides[3], center, 0.0))
                near_x.append(coef_x * (center[30:32] if forward else center[0:2]))
            for m, value in enumerate(five(second)):
                sums[ROW_SECOND + ROWS * m : ROW_SECOND + ROWS * (m + 1)] += value
            for m, value in enumerate(five(near_x)):
                at = ROW_SPILL_X + 4 * m + (0 if forward else 2)
                sums[at : at + 2] += value
            packed = sums[ROW_SPILL_Y : ROW_SPILL_Y + ROWS]
            for m, value in enumerate(five(near_y)):
                packed = packed + (pltpu.roll(value, 8 * m, 1) if m else value)
            sums[ROW_SPILL_Y : ROW_SPILL_Y + ROWS] = packed

            return carry

        lax.fori_loop(0, GROUPS, one, 0)

    sums[...] = jnp.zeros_like(sums)

    def both(forward):
        store = enter(forward)
        spread(forward)
        store.wait()

    each_sign(device >= 32, both)
    for m in range(5):
        at = ROW_EDGE + 4 * m
        sums[at : at + 2] = sums[ROWS * m + 30 : ROWS * m + 32]
        sums[at + 2 : at + 4] = sums[ROWS * m : ROWS * m + 2]

    @pl.when(device == 0)
    def _():
        at = ROW_EDGE + 20
        sums[at : at + 2] = rate[30:32]
        sums[at + 2 : at + 4] = rate[0:2]
        sums[ROW_RATE : ROW_RATE + ROWS] = rate[...]


def parameters(moments):
    density = moments[0]
    share = 1.0 / density
    flow_x = moments[1] * share
    flow_y = moments[2] * share
    flow_z = moments[3] * share
    temper = (moments[4] * share - (flow_x * flow_x + flow_y * flow_y + flow_z * flow_z)) / 3.0
    return density / (temper * jnp.sqrt(temper)), flow_x, flow_y, flow_z, 0.5 / temper


def products(part_x, part_y, part_z):
    yz = part_y[0] * part_z[0]
    return (
        part_x[0] * yz,
        part_x[1] * yz,
        part_x[0] * (part_y[1] * part_z[0]),
        part_x[0] * (part_y[0] * part_z[1]),
        part_x[2] * yz + part_x[0] * (part_y[2] * part_z[0] + part_y[0] * part_z[2]),
    )


def one_block(at, moments, rate, base, tables, kinds, wanted):
    amp, flow_x, flow_y, flow_z, inv = parameters(moments)
    scale = amp * rate
    base[at] = scale
    full, plus, minus = [], [], []
    for d, flow in enumerate((flow_x, flow_y, flow_z)):
        halves = []
        for half in range(2):
            level = [None] * 4
            for n in range(half * 10, half * 10 + 10):
                gap = SPEEDS[n] - flow
                value = jnp.exp(-(inv * gap * gap))
                tables[d, n, at] = value
                for k in range(4):
                    term = value if k == 0 else value * (SPEEDS[n] ** k)
                    level[k] = term if level[k] is None else level[k] + term
            halves.append(level)
        full.append([halves[0][k] + halves[1][k] for k in range(3)])
        plus.append([halves[1][k + 1] for k in range(3)])
        minus.append([-halves[0][k + 1] for k in range(3)])
    scale = scale * WEIGHT
    x, y, z = [scale * part for part in full[0]], full[1], full[2]
    sets = {}
    if "x" in wanted:
        sets[0] = products([scale * part for part in plus[0]], y, z)
        sets[1] = products([scale * part for part in minus[0]], y, z)
    if "y" in wanted:
        sets[2] = products(x, plus[1], z)
        sets[3] = products(x, minus[1], z)
    if "z" in wanted:
        sets[4] = products(x, y, [plus[2][k] + minus[2][k] for k in range(3)])
        whole = products(x, y, z)
        sets[5] = [
            whole[m]
            - (1.5 * DT) * ((sets[0][m] + sets[1][m]) + (sets[2][m] + sets[3][m]))
            - (2.0 * DT) * sets[4][m]
            for m in range(5)
        ]
    for s, values in sets.items():
        for m in range(5):
            kinds[s, m, at] = values[m]


def table_kernel(wanted, total, rate, base, tables, kinds):
    def block(b, carry):
        def rows(start):
            return pl.ds(pl.multiple_of(start + b * 8, 8), 8)

        one_block(
            rows(0), [total[rows(ROWS * m)] for m in range(5)], rate[rows(0)], base, tables, kinds,
            wanted,
        )
        return carry

    lax.fori_loop(0, ROWS // 8, block, 0)


def second_inside_kernel(
    place, kept, kept_near, base, tables, base_near, tables_near, moved_part, held_near, sem
):
    for piece in range(STEPS):
        load_piece(kept_near, held_near, sem, piece).start()
    device = place[0]
    first = device * VEL_LOCAL
    even = lax.rem(lane_index(), 2) == 0

    def move(forward):
        def chunk(c, carry):
            group, index_x, index_y, index_z = chunk_place(first, c)
            coef_x = DT * jnp.abs(speed_of(index_x))
            coef_y = DT * jnp.abs(speed_of(index_y))
            side = jnp.where(index_z >= VG // 2, 1.0, -1.0)
            sides = y_sides(index_y >= VG // 2)
            front = base[...] * tables[0, index_x] * tables[1, index_y]
            front_near = base_near[...] * tables_near[0, index_x] * tables_near[1, index_y]
            at = [c * CHUNK + t for t in range(CHUNK)]
            centers = [kept[v] + front * tables[2, index_z + t] for t, v in enumerate(at)]
            nears = [
                held_near[v] + front_near * tables_near[2, index_z + t] for t, v in enumerate(at)
            ]
            backs = [y_part(center, near, sides) for center, near in zip(centers, nears)]
            for t, v in enumerate(at):
                moved_part[v] = upwind(
                    centers[t], backs[t], *x_inside(centers[t], forward), even, coef_x, coef_y,
                    DT * speed_of(index_z + t) * side,
                )
            return carry

        def piece(p, carry):
            load_piece(kept_near, held_near, sem, p).wait()
            for c in range(STEP_CHUNKS):
                chunk(p * STEP_CHUNKS + c, carry)
            return carry

        lax.fori_loop(0, STEPS, piece, 0)

    each_sign(device >= 32, move)


def second_kernel(
    place, moved_part, kept_edge, total, total_near, total_edge, rate, kinds, kinds_near,
    out, base_edge, tables_edge, kinds_edge, table_two, done, buf, sem,
):
    device = place[0]
    first = device * VEL_LOCAL
    even = lax.rem(lane_index(), 2) == 0
    keep = 1.0 - rate[...]

    def edge(row):
        rows = total_edge[row : row + 4]
        return jnp.concatenate([rows, rows], axis=0)

    one_block(
        slice(0, 8), [edge(ROWS + 4 * m) for m in range(5)], edge(ROWS + 20), base_edge,
        tables_edge, kinds_edge, "x",
    )
    spill_y = total_near[ROW_SPILL_Y : ROW_SPILL_Y + ROWS]
    moments = []
    for m in range(5):
        result = total[ROW_SECOND + ROWS * m : ROW_SECOND + ROWS * (m + 1)] + kinds[5, m]
        x_one, x_two = x_steps(
            buf, 0, kinds[0, m],
            kinds_edge[0, m, 0:2] + (1.0 / DT) * total_edge[4 * m : 4 * m + 2], True,
        )
        x_low, x_lower = x_steps(
            buf, 1, kinds[1, m],
            kinds_edge[1, m, 2:4] + (1.0 / DT) * total_edge[4 * m + 2 : 4 * m + 4], False,
        )
        spill = pltpu.roll(spill_y, LANES - 8 * m, 1) if m else spill_y
        spill = (1.0 / DT) * spill
        moments.append(
            result
            + (2.0 * DT)
            * (
                other_plane(kinds[4, m], even)
                + (x_one - 0.25 * x_two)
                + (x_low - 0.25 * x_lower)
                + y_part(kinds[2, m], kinds_near[2, m] + spill, y_sides(True))
                + y_part(kinds[3, m], kinds_near[3, m] + spill, y_sides(False))
            )
        )
    amp, flow_x, flow_y, flow_z, inv = parameters(moments)
    for n in range(VG):
        gap = SPEEDS[n] - flow_z
        table_two[n] = jnp.exp(-(inv * gap * gap))
    table_two[VG] = amp * rate[...]
    table_two[VG + 1] = flow_x
    table_two[VG + 2] = flow_y
    table_two[VG + 3] = inv


    def move(forward):
        row = 0 if forward else 2
        rows = slice(0, 2) if forward else slice(30, 32)
        none = jnp.zeros((1, LANES), jnp.float32)

        def chunk(c, carry):
            group, index_x, index_y, index_z = chunk_place(first, c)
            speed_x = speed_of(index_x)
            coef = (2.0 * DT) * jnp.abs(speed_x)
            gap_x = speed_x - table_two[VG + 1]
            gap_y = speed_of(index_y) - table_two[VG + 2]
            front_two = table_two[VG] * jnp.exp(
                -(table_two[VG + 3] * (gap_x * gap_x + gap_y * gap_y))
            )
            front_edge = base_edge[...] * tables_edge[0, index_x] * tables_edge[1, index_y]
            for t in range(CHUNK):
                v = c * CHUNK + t
                n = index_z + t
                halo = kept_edge[v] + (front_edge * tables_edge[2, n])[row : row + 2]
                one = [halo[1:2], none] if forward else [none, halo[0:1]]
                entered = coef * (jnp.concatenate(one, axis=0) - 0.25 * halo)
                done[v] = keep * moved_part[v] + front_two * table_two[n]
                done[v, rows] += keep[rows] * entered
            return carry

        def piece(p, carry):
            for c in range(STEP_CHUNKS):
                chunk(p * STEP_CHUNKS + c, carry)
            load_piece(done, out, sem, p).start()
            return carry

        lax.fori_loop(0, STEPS, piece, 0)

    each_sign(device >= 32, move)
    for piece in range(STEPS):
        load_piece(done, out, sem, piece).wait()


def vmem():
    return pl.BlockSpec(memory_space=pltpu.VMEM)


def in_hbm(x):
    return pltpu.with_memory_space_constraint(x, pltpu.HBM)


def hbm():
    return pl.BlockSpec(memory_space=pltpu.HBM)


def anywhere():
    return pl.BlockSpec(memory_space=pl.ANY)


def smem():
    return pl.BlockSpec(memory_space=pltpu.SMEM)


SWAP = [(0, 1), (1, 0)]


def sum_over_vert(partial, beside):
    parts = partial.reshape(8, -1, 8, LANES)
    share = jnp.sum(lax.all_to_all(parts, PLANE, 0, 0), axis=0)
    share = jnp.sum(lax.all_to_all(jnp.broadcast_to(share[None], parts.shape), "z", 0, 0), axis=0)
    share, beside = lax.optimization_barrier((share, beside))
    whole = lax.all_to_all(jnp.broadcast_to(share[None], parts.shape), PLANE, 0, 0)
    return whole.reshape(ROW_COUNT, LANES), beside


def f32(*shape):
    return jax.ShapeDtypeStruct(shape, jnp.float32)


def tables_of(total, rate, wanted, name):
    return pl.pallas_call(
        functools.partial(table_kernel, wanted),
        out_shape=(
            f32(ROWS, LANES), f32(3, VG, ROWS, LANES), f32(6, 5, ROWS, LANES)
        ),
        in_specs=[vmem(), vmem()],
        out_specs=(vmem(), vmem(), vmem()),
        compiler_params=pltpu.CompilerParams(vmem_limit_bytes=16 * 2**20),
        cost_estimate=pl.CostEstimate(flops=8000000, bytes_accessed=3000000, transcendentals=250000),
        name=name,
    )(total, rate)


def body(distribution, collision_rate):
    device = lax.axis_index(VERT)
    place = device.astype(jnp.int32).reshape(1)
    f_edge = pl.pallas_call(
        send_kernel,
        out_shape=f32(VEL_LOCAL, 2, LANES),
        in_specs=[smem(), hbm()],
        out_specs=vmem(),
        scratch_shapes=[pltpu.VMEM((VEL_LOCAL, 8, LANES), jnp.float32), pltpu.SemaphoreType.DMA],
        compiler_params=pltpu.CompilerParams(vmem_limit_bytes=24 * 2**20),
        cost_estimate=pl.CostEstimate(flops=0, bytes_accessed=600000, transcendentals=0),
        name="send_rows",
    )(place, in_hbm(distribution))
    f_edge = lax.ppermute(f_edge, "gx", SWAP)
    f_near = lax.ppermute(distribution, "gy", SWAP)
    kept, kept_edge, groups = pl.pallas_call(
        inside_kernel,
        out_shape=(
            f32(VEL_LOCAL, ROWS, LANES), f32(VEL_LOCAL, 2, LANES), f32(GROUPS, 6, ROWS, LANES)
        ),
        in_specs=[smem(), hbm(), hbm(), hbm()],
        out_specs=(vmem(), vmem(), vmem()),
        scratch_shapes=[
            pltpu.VMEM((VEL_LOCAL, ROWS, LANES), jnp.float32),
            pltpu.VMEM((VEL_LOCAL, ROWS, LANES), jnp.float32),
            pltpu.VMEM((ROWS, LANES), jnp.float32),
            pltpu.SemaphoreType.DMA((STEPS,)),
            pltpu.SemaphoreType.DMA((STEPS,)),
            pltpu.SemaphoreType.DMA,
        ],
        compiler_params=pltpu.CompilerParams(vmem_limit_bytes=16 * 2**20),
        cost_estimate=pl.CostEstimate(flops=50000000, bytes_accessed=6000000, transcendentals=0),
        name="move_inside",
    )(place, in_hbm(distribution), in_hbm(f_near), in_hbm(collision_rate))
    kept_edge = lax.ppermute(kept_edge, "gx", SWAP)
    kept, partial = pl.pallas_call(
        edge_kernel,
        out_shape=(f32(VEL_LOCAL, ROWS, LANES), f32(ROW_COUNT, LANES)),
        in_specs=[smem(), anywhere()] + [vmem()] * 3,
        out_specs=(anywhere(), vmem()),
        scratch_shapes=[
            pltpu.VMEM((GROUPS, 6, ROWS, LANES), jnp.float32),
            pltpu.VMEM((VEL_LOCAL, 8, LANES), jnp.float32),
            pltpu.VMEM((CHUNK, 48, LANES), jnp.float32),
            pltpu.SemaphoreType.DMA,
        ],
        input_output_aliases={1: 0},
        compiler_params=pltpu.CompilerParams(vmem_limit_bytes=16 * 2**20),
        name="enter_and_sum",
    )(place, kept, groups, f_edge, collision_rate)
    kept_near = lax.ppermute(kept, "gy", SWAP)
    total, kept_edge = sum_over_vert(partial, kept_edge)
    total_near = lax.ppermute(total, "gy", SWAP)
    total_edge = lax.ppermute(total[ROW_SPILL_X : ROW_EDGE + ROWS], "gx", SWAP)
    own = tables_of(total, collision_rate, "xyz", "tables_own")
    near = tables_of(total_near, total_near[ROW_RATE : ROW_RATE + ROWS], "y", "tables_near")
    moved_part = pl.pallas_call(
        second_inside_kernel,
        out_shape=f32(VEL_LOCAL, ROWS, LANES),
        in_specs=[smem(), vmem(), hbm()] + [vmem()] * 4,
        out_specs=vmem(),
        scratch_shapes=[
            pltpu.VMEM((VEL_LOCAL, ROWS, LANES), jnp.float32),
            pltpu.SemaphoreType.DMA((STEPS,)),
        ],
        compiler_params=pltpu.CompilerParams(vmem_limit_bytes=16 * 2**20),
        cost_estimate=pl.CostEstimate(flops=50000000, bytes_accessed=6000000, transcendentals=0),
        name="move_inside_two",
    )(place, kept, in_hbm(kept_near), *own[:2], *near[:2])
    return pl.pallas_call(
        second_kernel,
        out_shape=f32(VEL_LOCAL, ROWS, LANES),
        in_specs=[smem()] + [vmem()] * 8,
        out_specs=anywhere(),
        scratch_shapes=[
            pltpu.VMEM((8, LANES), jnp.float32),
            pltpu.VMEM((3, VG, 8, LANES), jnp.float32),
            pltpu.VMEM((2, 5, 8, LANES), jnp.float32),
            pltpu.VMEM((VG + 4, ROWS, LANES), jnp.float32),
            pltpu.VMEM((VEL_LOCAL, ROWS, LANES), jnp.float32),
            pltpu.VMEM((CHUNK, 48, LANES), jnp.float32),
            pltpu.SemaphoreType.DMA((STEPS,)),
        ],
        compiler_params=pltpu.CompilerParams(vmem_limit_bytes=24 * 2**20),
        name="collide_two",
    )(
        place, moved_part, kept_edge, total, total_near, total_edge, collision_rate, own[2],
        near[2],
    )


def solution(mesh):
    split = Mesh(mesh.devices.reshape(2, 2, 4, 2, 8), ("gx", "gy", "x", "yl", "z"))
    placed = (P(VERT, "gx", "gy"), P("gx", "gy"))
    return jax.shard_map(
        body, mesh=split, in_specs=placed, out_specs=P(VERT, "gx", "gy"), check_vma=False
    )
```

```python
import functools
import math

import jax
import jax.numpy as jnp
from jax import lax
from jax.experimental import pallas as pl
from jax.experimental.pallas import tpu as pltpu
from jax.sharding import Mesh
from jax.sharding import PartitionSpec as P

VG = 20
VEL_LOCAL = 125
CHUNK = 5
CHUNKS = VEL_LOCAL // CHUNK
STEPS = 5
STEP_CHUNKS = CHUNKS // STEPS
PIECE = VEL_LOCAL // STEPS
GROUPS = 7
ROWS = 32
LANES = 128

SPACING = 9.0 / VG
LOWEST = 4.5 * (1.0 / VG - 1.0)
DT = 0.3 / 4.5
WEIGHT = (9.0 / VG) ** 3 / (2.0 * math.pi) ** 1.5
SPEEDS = [LOWEST + SPACING * n for n in range(VG)]

VERT = ("x", "yl", "z")
PLANE = ("x", "yl")

ROW_SECOND = 5 * ROWS
ROW_PACKED = 10 * ROWS
ROW_SPILL_X = 11 * ROWS
ROW_EDGE = ROW_SPILL_X + 20
ROW_COUNT = 12 * ROWS
HALF = LANES // 2
HALF_AT = 48
FEW = 12


def speed_of(index):
    return index.astype(jnp.float32) * SPACING + LOWEST


def lane_index():
    return lax.broadcasted_iota(jnp.int32, (ROWS, LANES), 1)


def other_plane(tile, even):
    return jnp.where(even, pltpu.roll(tile, LANES - 1, 1), pltpu.roll(tile, 1, 1))


def chunk_place(first, chunk):
    slot = lax.rem(first, VG) + chunk * CHUNK
    group = lax.div(slot, VG)
    whole = lax.div(first, VG) + group
    index_x = lax.div(whole, VG)
    return group, index_x, whole - index_x * VG, slot - group * VG


def y_sides(positive):
    lane = lane_index()
    if positive is True:
        return 2, 4, lane >= LANES - 2, lane >= LANES - 4
    if positive is False:
        return LANES - 2, LANES - 4, lane < 2, lane < 4
    one = ((lane + jnp.where(positive, 2, 0)) & (LANES - 1)) < 2
    two = ((lane + jnp.where(positive, 4, 0)) & (LANES - 1)) < 4
    return jnp.where(positive, 2, LANES - 2), jnp.where(positive, 4, LANES - 4), one, two


def y_part(center, near, sides):
    shift_one, shift_two, one, two = sides
    return pltpu.roll(jnp.where(one, near, center), shift_one, 1) - 0.25 * pltpu.roll(
        jnp.where(two, near, center), shift_two, 1
    )


def upwind(center, back, x_one, x_two, even, coef_x, coef_y, coef_z):
    return (
        center * (1.0 - 1.5 * (coef_x + coef_y) - 2.0 * coef_z)
        + (2.0 * coef_x) * (x_one - 0.25 * x_two)
        + (2.0 * coef_y) * back
        + (2.0 * coef_z) * other_plane(center, even)
    )


def each_sign(positive, run):
    for value in (True, False):
        pl.when(positive if value else jnp.logical_not(positive))(functools.partial(run, value))


def x_steps(buf, slot, center, halo, forward):
    buf[slot, 8:40] = center
    if forward:
        buf[slot, 6:8] = halo
        return buf[slot, 7:39], buf[slot, 6:38]
    buf[slot, 40:42] = halo
    return buf[slot, 9:41], buf[slot, 10:42]


def load_piece(f, held, sem, piece):
    rows = pl.ds(piece * PIECE, PIECE)
    return pltpu.make_async_copy(f.at[rows], held.at[rows], sem.at[piece])


def x_inside(center, forward):
    row = lax.broadcasted_iota(jnp.int32, (ROWS, LANES), 0)
    if forward:
        return [jnp.where(row >= n, pltpu.roll(center, n, 0), 0.0) for n in (1, 2)]
    return [jnp.where(row < ROWS - n, pltpu.roll(center, ROWS - n, 0), 0.0) for n in (1, 2)]


def send_kernel(place, f, out, band, sem):
    def take(forward):
        copy = pltpu.make_async_copy(f.at[:, pl.ds(24 if forward else 0, 8)], band, sem)
        copy.start()
        copy.wait()
        out[...] = band[:, 6:8] if forward else band[:, 0:2]

    each_sign(place[0] >= 32, take)


def inside_kernel(
    place, f, f_near, rate, kept, kept_edge, groups, held, held_near, held_rate, sem, sem_near,
    sem_rate,
):
    rate_copy = pltpu.make_async_copy(rate, held_rate, sem_rate)
    rate_copy.start()
    for piece in range(STEPS):
        load_piece(f, held, sem, piece).start()
        load_piece(f_near, held_near, sem_near, piece).start()
    rate_copy.wait()
    device = place[0]
    first = device * VEL_LOCAL
    even = lax.rem(lane_index(), 2) == 0
    keep = 1.0 - held_rate[...]
    groups[...] = jnp.zeros_like(groups)

    def move(forward):
        def chunk(c, carry):
            group, index_x, index_y, index_z = chunk_place(first, c)
            coef_x = DT * jnp.abs(speed_of(index_x))
            coef_y = DT * jnp.abs(speed_of(index_y))
            side = jnp.where(index_z >= VG // 2, 1.0, -1.0)

            sides = y_sides(index_y >= VG // 2)
            acc = [None] * 4
            at = [c * CHUNK + t for t in range(CHUNK)]
            speeds = [speed_of(index_z + t) for t in range(CHUNK)]
            centers = [held[v] for v in at]
            nears = [held_near[v] for v in at]
            backs = [y_part(center, near, sides) for center, near in zip(centers, nears)]
            moved = [
                upwind(center, back, *x_inside(center, forward), even, coef_x, coef_y,
                       DT * speed * side)
                for center, back, speed in zip(centers, backs, speeds)
            ]
            for value, speed in zip(moved, speeds):
                power = value
                for k in range(4):
                    acc[k] = power if acc[k] is None else acc[k] + power
                    if k < 3:
                        power = power * speed
            for v, value in zip(at, moved):
                left = keep * value
                kept[v] = left
                kept_edge[v] = left[30:32] if forward else left[0:2]
            for k in range(3):
                groups[group, k] += acc[k]
                groups[group, 3 + k] += side * acc[k + 1]

            return carry

        def piece(p, carry):
            load_piece(f, held, sem, p).wait()
            load_piece(f_near, held_near, sem_near, p).wait()
            for c in range(STEP_CHUNKS):
                chunk(p * STEP_CHUNKS + c, carry)
            return carry

        lax.fori_loop(0, STEPS, piece, 0)

    each_sign(device >= 32, move)


def edge_kernel(
    place, kept_in, groups_in, f_edge, rate, kept, sums, groups, edge, few, buf, sem
):
    del kept_in
    device = place[0]
    first = device * VEL_LOCAL
    groups[...] = groups_in[...]
    even = lax.rem(lane_index(), 2) == 0
    keep = 1.0 - rate[...]

    def enter(forward):
        rows = slice(0, 2) if forward else slice(30, 32)
        inner = slice(0, 2) if forward else slice(6, 8)
        none = jnp.zeros((1, LANES), jnp.float32)
        band = kept.at[:, pl.ds(0 if forward else 24, 8)]
        load = pltpu.make_async_copy(band, edge, sem)
        load.start()
        load.wait()

        def chunk(c, carry):
            group, index_x, _, index_z = chunk_place(first, c)
            coef = (2.0 * DT) * jnp.abs(speed_of(index_x))
            side = jnp.where(index_z >= VG // 2, 1.0, -1.0)
            acc = [None] * 4
            for t in range(CHUNK):
                v = c * CHUNK + t
                halo = f_edge[v]
                one = [halo[1:2], none] if forward else [none, halo[0:1]]
                power = coef * (jnp.concatenate(one, axis=0) - 0.25 * halo)
                edge[v, inner] += keep[rows] * power
                speed_z = speed_of(index_z + t)
                for k in range(4):
                    acc[k] = power if acc[k] is None else acc[k] + power
                    if k < 3:
                        power = power * speed_z
            for k in range(3):
                groups[group, k, rows] += acc[k]
                groups[group, 3 + k, rows] += side * acc[k + 1]
            return carry

        def some(p, carry):
            for c in range(STEP_CHUNKS):
                chunk(p * STEP_CHUNKS + c, carry)
            return carry

        lax.fori_loop(0, STEPS, some, 0)
        store = pltpu.make_async_copy(edge, band, sem)
        store.start()
        return store

    def spread(forward):
        def one(group, carry):
            whole = lax.div(first, VG) + group
            index_x = lax.div(whole, VG)
            index_y = whole - index_x * VG
            speed_x = speed_of(index_x)
            speed_y = speed_of(index_y)
            coef_x = DT * jnp.abs(speed_x)
            coef_y = DT * jnp.abs(speed_y)
            squares = speed_x * speed_x + speed_y * speed_y

            def five(parts):
                return (
                    parts[0],
                    speed_x * parts[0],
                    speed_y * parts[0],
                    parts[1],
                    squares * parts[0] + parts[2],
                )

            sides = y_sides(index_y >= VG // 2)
            level = [WEIGHT * groups[group, k] for k in range(6)]
            for m, value in enumerate(five(level)):
                sums[ROWS * m : ROWS * (m + 1)] += value
            second, near_y, near_x = [], [], []
            for k in range(3):
                center = keep * level[k]
                absolute = keep * level[3 + k]
                x_one, x_two = x_steps(
                    buf, k, center, jnp.zeros((2, LANES), jnp.float32), forward
                )
                second.append(
                    center * (1.0 - 1.5 * (coef_x + coef_y))
                    - (2.0 * DT) * (absolute - other_plane(absolute, even))
                    + (2.0 * coef_x) * (x_one - 0.25 * x_two)
                    + (2.0 * coef_y) * y_part(center, 0.0, sides)
                )
                near_y.append(coef_y * jnp.where(sides[3], center, 0.0))
                near_x.append(coef_x * (center[30:32] if forward else center[0:2]))
            for m, value in enumerate(five(second)):
                sums[ROW_SECOND + ROWS * m : ROW_SECOND + ROWS * (m + 1)] += value
            for m, value in enumerate(five(near_x)):
                at = ROW_SPILL_X + 4 * m + (0 if forward else 2)
                sums[at : at + 2] += value
            packed = sums[ROW_PACKED : ROW_PACKED + ROWS]
            for m, value in enumerate(five(near_y)):
                packed = packed + (pltpu.roll(value, 8 * m, 1) if m else value)
            sums[ROW_PACKED : ROW_PACKED + ROWS] = packed

            return carry

        lax.fori_loop(0, GROUPS, one, 0)

    sums[...] = jnp.zeros_like(sums)

    def both(forward):
        store = enter(forward)
        spread(forward)
        store.wait()

    each_sign(device >= 32, both)
    for m in range(5):
        target, at = (sums, ROW_EDGE + 4 * m) if m < 3 else (few, 4 * (m - 3))
        target[at : at + 2] = sums[ROWS * m + 30 : ROWS * m + 32]
        target[at + 2 : at + 4] = sums[ROWS * m : ROWS * m + 2]
    few[8:16] = jnp.zeros((8, LANES), jnp.float32)

    @pl.when(device == 0)
    def _():
        few[8:10] = rate[30:32]
        few[10:12] = rate[0:2]
        lane = lane_index()
        border = jnp.where((lane < 4) | (lane >= LANES - 4), rate[...], 0.0)
        sums[ROW_PACKED : ROW_PACKED + ROWS] += pltpu.roll(border, 40, 1)

    rest = few[...]
    lane = lax.broadcasted_iota(jnp.int32, rest.shape, 1)
    left = pltpu.roll(jnp.where(lane < HALF, rest, 0.0), HALF_AT, 1)
    right = pltpu.roll(jnp.where(lane >= HALF, rest, 0.0), LANES - (HALF - HALF_AT), 1)
    sums[ROW_PACKED : ROW_PACKED + FEW] += left[0:FEW]
    sums[ROW_PACKED + FEW : ROW_PACKED + 2 * FEW] += right[0:FEW]


def parameters(moments):
    density = moments[0]
    share = 1.0 / density
    flow_x = moments[1] * share
    flow_y = moments[2] * share
    flow_z = moments[3] * share
    temper = (moments[4] * share - (flow_x * flow_x + flow_y * flow_y + flow_z * flow_z)) / 3.0
    return density / (temper * jnp.sqrt(temper)), flow_x, flow_y, flow_z, 0.5 / temper


def products(part_x, part_y, part_z):
    yz = part_y[0] * part_z[0]
    return (
        part_x[0] * yz,
        part_x[1] * yz,
        part_x[0] * (part_y[1] * part_z[0]),
        part_x[0] * (part_y[0] * part_z[1]),
        part_x[2] * yz + part_x[0] * (part_y[2] * part_z[0] + part_y[0] * part_z[2]),
    )


def one_block(at, moments, rate, base, tables, kinds, wanted):
    amp, flow_x, flow_y, flow_z, inv = parameters(moments)
    scale = amp * rate
    base[at] = scale
    full, plus, minus = [], [], []
    for d, flow in enumerate((flow_x, flow_y, flow_z)):
        halves = []
        for half in range(2):
            level = [None] * 4
            for n in range(half * 10, half * 10 + 10):
                gap = SPEEDS[n] - flow
                value = jnp.exp(-(inv * gap * gap))
                tables[d, n, at] = value
                for k in range(4):
                    term = value if k == 0 else value * (SPEEDS[n] ** k)
                    level[k] = term if level[k] is None else level[k] + term
            halves.append(level)
        full.append([halves[0][k] + halves[1][k] for k in range(3)])
        plus.append([halves[1][k + 1] for k in range(3)])
        minus.append([-halves[0][k + 1] for k in range(3)])
    scale = scale * WEIGHT
    x, y, z = [scale * part for part in full[0]], full[1], full[2]
    sets = {}
    if "x" in wanted:
        sets[0] = products([scale * part for part in plus[0]], y, z)
        sets[1] = products([scale * part for part in minus[0]], y, z)
    if "y" in wanted:
        sets[2] = products(x, plus[1], z)
        sets[3] = products(x, minus[1], z)
    if "z" in wanted:
        sets[4] = products(x, y, [plus[2][k] + minus[2][k] for k in range(3)])
        whole = products(x, y, z)
        sets[5] = [
            whole[m]
            - (1.5 * DT) * ((sets[0][m] + sets[1][m]) + (sets[2][m] + sets[3][m]))
            - (2.0 * DT) * sets[4][m]
            for m in range(5)
        ]
    for s, values in sets.items():
        for m in range(5):
            kinds[s, m, at] = values[m]


def table_kernel(wanted, total, rate, base, tables, kinds):
    for at in range(0, ROWS, 8):
        rows = slice(at, at + 8)
        one_block(
            rows, [total[ROWS * m + at : ROWS * m + at + 8] for m in range(5)], rate[rows], base,
            tables, kinds, wanted,
        )


def near_kernel(wanted, total, base, tables, kinds):
    for at in range(0, ROWS, 8):
        rate = pltpu.roll(total[ROW_PACKED + at : ROW_PACKED + at + 8], LANES - 40, 1)
        one_block(
            slice(at, at + 8), [total[ROWS * m + at : ROWS * m + at + 8] for m in range(5)], rate,
            base, tables, kinds, wanted,
        )


def second_inside_kernel(
    place, kept, kept_near, base, tables, base_near, tables_near, moved_part, held_near, sem
):
    for piece in range(STEPS):
        load_piece(kept_near, held_near, sem, piece).start()
    device = place[0]
    first = device * VEL_LOCAL
    even = lax.rem(lane_index(), 2) == 0

    def move(forward):
        def chunk(c, carry):
            group, index_x, index_y, index_z = chunk_place(first, c)
            coef_x = DT * jnp.abs(speed_of(index_x))
            coef_y = DT * jnp.abs(speed_of(index_y))
            side = jnp.where(index_z >= VG // 2, 1.0, -1.0)
            sides = y_sides(index_y >= VG // 2)
            front = base[...] * tables[0, index_x] * tables[1, index_y]
            front_near = base_near[...] * tables_near[0, index_x] * tables_near[1, index_y]
            at = [c * CHUNK + t for t in range(CHUNK)]
            centers = [kept[v] + front * tables[2, index_z + t] for t, v in enumerate(at)]
            nears = [
                held_near[v] + front_near * tables_near[2, index_z + t] for t, v in enumerate(at)
            ]
            backs = [y_part(center, near, sides) for center, near in zip(centers, nears)]
            for t, v in enumerate(at):
                moved_part[v] = upwind(
                    centers[t], backs[t], *x_inside(centers[t], forward), even, coef_x, coef_y,
                    DT * speed_of(index_z + t) * side,
                )
            return carry

        def piece(p, carry):
            load_piece(kept_near, held_near, sem, p).wait()
            for c in range(STEP_CHUNKS):
                chunk(p * STEP_CHUNKS + c, carry)
            return carry

        lax.fori_loop(0, STEPS, piece, 0)

    each_sign(device >= 32, move)


def second_kernel(
    place, moved_part, kept_edge, total, total_near, total_edge, rate, kinds, kinds_near,
    out, base_edge, tables_edge, kinds_edge, table_two, done, few, buf, sem,
):
    device = place[0]
    first = device * VEL_LOCAL
    even = lax.rem(lane_index(), 2) == 0
    keep = 1.0 - rate[...]

    left = pltpu.roll(total_edge[0:16], LANES - HALF_AT, 1)
    right = pltpu.roll(total_edge[FEW : FEW + 16], HALF - HALF_AT, 1)
    few[...] = jnp.where(lax.broadcasted_iota(jnp.int32, left.shape, 1) < HALF, left, right)

    def edge(source, row):
        rows = source[row : row + 4]
        return jnp.concatenate([rows, rows], axis=0)

    one_block(
        slice(0, 8),
        [edge(total_edge, ROWS + 20 + 4 * m) for m in range(3)] + [edge(few, 0), edge(few, 4)],
        edge(few, 8), base_edge,
        tables_edge, kinds_edge, "x",
    )
    spill_y = total_near[ROW_PACKED : ROW_PACKED + ROWS]
    moments = []
    for m in range(5):
        result = total[ROW_SECOND + ROWS * m : ROW_SECOND + ROWS * (m + 1)] + kinds[5, m]
        x_one, x_two = x_steps(
            buf, 0, kinds[0, m],
            kinds_edge[0, m, 0:2] + (1.0 / DT) * total_edge[ROWS + 4 * m : ROWS + 4 * m + 2], True,
        )
        x_low, x_lower = x_steps(
            buf, 1, kinds[1, m],
            kinds_edge[1, m, 2:4] + (1.0 / DT) * total_edge[ROWS + 4 * m + 2 : ROWS + 4 * m + 4], False,
        )
        spill = pltpu.roll(spill_y, LANES - 8 * m, 1) if m else spill_y
        spill = (1.0 / DT) * spill
        moments.append(
            result
            + (2.0 * DT)
            * (
                other_plane(kinds[4, m], even)
                + (x_one - 0.25 * x_two)
                + (x_low - 0.25 * x_lower)
                + y_part(kinds[2, m], kinds_near[2, m] + spill, y_sides(True))
                + y_part(kinds[3, m], kinds_near[3, m] + spill, y_sides(False))
            )
        )
    amp, flow_x, flow_y, flow_z, inv = parameters(moments)
    for n in range(VG):
        gap = SPEEDS[n] - flow_z
        table_two[n] = jnp.exp(-(inv * gap * gap))
    table_two[VG] = amp * rate[...]
    table_two[VG + 1] = flow_x
    table_two[VG + 2] = flow_y
    table_two[VG + 3] = inv


    def move(forward):
        row = 0 if forward else 2
        rows = slice(0, 2) if forward else slice(30, 32)
        none = jnp.zeros((1, LANES), jnp.float32)

        def chunk(c, carry):
            group, index_x, index_y, index_z = chunk_place(first, c)
            speed_x = speed_of(index_x)
            coef = (2.0 * DT) * jnp.abs(speed_x)
            gap_x = speed_x - table_two[VG + 1]
            gap_y = speed_of(index_y) - table_two[VG + 2]
            front_two = table_two[VG] * jnp.exp(
                -(table_two[VG + 3] * (gap_x * gap_x + gap_y * gap_y))
            )
            front_edge = base_edge[...] * tables_edge[0, index_x] * tables_edge[1, index_y]
            for t in range(CHUNK):
                v = c * CHUNK + t
                n = index_z + t
                halo = kept_edge[v] + (front_edge * tables_edge[2, n])[row : row + 2]
                one = [halo[1:2], none] if forward else [none, halo[0:1]]
                entered = coef * (jnp.concatenate(one, axis=0) - 0.25 * halo)
                done[v] = keep * moved_part[v] + front_two * table_two[n]
                done[v, rows] += keep[rows] * entered
            return carry

        def piece(p, carry):
            for c in range(STEP_CHUNKS):
                chunk(p * STEP_CHUNKS + c, carry)
            load_piece(done, out, sem, p).start()
            return carry

        lax.fori_loop(0, STEPS, piece, 0)

    each_sign(device >= 32, move)
    for piece in range(STEPS):
        load_piece(done, out, sem, piece).wait()


def vmem():
    return pl.BlockSpec(memory_space=pltpu.VMEM)


def in_hbm(x):
    return pltpu.with_memory_space_constraint(x, pltpu.HBM)


def hbm():
    return pl.BlockSpec(memory_space=pltpu.HBM)


def anywhere():
    return pl.BlockSpec(memory_space=pl.ANY)


def smem():
    return pl.BlockSpec(memory_space=pltpu.SMEM)


SWAP = [(0, 1), (1, 0)]


def sum_over_vert(partial, beside):
    parts = partial.reshape(8, -1, 8, LANES)
    share = jnp.sum(lax.all_to_all(parts, PLANE, 0, 0), axis=0)
    share = jnp.sum(lax.all_to_all(jnp.broadcast_to(share[None], parts.shape), "z", 0, 0), axis=0)
    share, beside = lax.optimization_barrier((share, beside))
    whole = lax.all_to_all(jnp.broadcast_to(share[None], parts.shape), PLANE, 0, 0)
    return whole.reshape(ROW_COUNT, LANES), beside


def f32(*shape):
    return jax.ShapeDtypeStruct(shape, jnp.float32)


def tables_of(kernel, wanted, name, *operands):
    return pl.pallas_call(
        functools.partial(kernel, wanted),
        out_shape=(
            f32(ROWS, LANES), f32(3, VG, ROWS, LANES), f32(6, 5, ROWS, LANES)
        ),
        in_specs=[vmem()] * len(operands),
        out_specs=(vmem(), vmem(), vmem()),
        compiler_params=pltpu.CompilerParams(vmem_limit_bytes=16 * 2**20),
        cost_estimate=pl.CostEstimate(flops=8000000, bytes_accessed=3000000, transcendentals=250000),
        name=name,
    )(*operands)


def body(distribution, collision_rate):
    device = lax.axis_index(VERT)
    place = device.astype(jnp.int32).reshape(1)
    f_edge = pl.pallas_call(
        send_kernel,
        out_shape=f32(VEL_LOCAL, 2, LANES),
        in_specs=[smem(), hbm()],
        out_specs=vmem(),
        scratch_shapes=[pltpu.VMEM((VEL_LOCAL, 8, LANES), jnp.float32), pltpu.SemaphoreType.DMA],
        compiler_params=pltpu.CompilerParams(vmem_limit_bytes=24 * 2**20),
        cost_estimate=pl.CostEstimate(flops=0, bytes_accessed=600000, transcendentals=0),
        name="send_rows",
    )(place, in_hbm(distribution))
    f_edge = lax.ppermute(f_edge, "gx", SWAP)
    f_near = lax.ppermute(distribution, "gy", SWAP)
    kept, kept_edge, groups = pl.pallas_call(
        inside_kernel,
        out_shape=(
            f32(VEL_LOCAL, ROWS, LANES), f32(VEL_LOCAL, 2, LANES), f32(GROUPS, 6, ROWS, LANES)
        ),
        in_specs=[smem(), hbm(), hbm(), hbm()],
        out_specs=(vmem(), vmem(), vmem()),
        scratch_shapes=[
            pltpu.VMEM((VEL_LOCAL, ROWS, LANES), jnp.float32),
            pltpu.VMEM((VEL_LOCAL, ROWS, LANES), jnp.float32),
            pltpu.VMEM((ROWS, LANES), jnp.float32),
            pltpu.SemaphoreType.DMA((STEPS,)),
            pltpu.SemaphoreType.DMA((STEPS,)),
            pltpu.SemaphoreType.DMA,
        ],
        compiler_params=pltpu.CompilerParams(vmem_limit_bytes=16 * 2**20),
        cost_estimate=pl.CostEstimate(flops=50000000, bytes_accessed=6000000, transcendentals=0),
        name="move_inside",
    )(place, in_hbm(distribution), in_hbm(f_near), in_hbm(collision_rate))
    kept_edge = lax.ppermute(kept_edge, "gx", SWAP)
    kept, partial = pl.pallas_call(
        edge_kernel,
        out_shape=(f32(VEL_LOCAL, ROWS, LANES), f32(ROW_COUNT, LANES)),
        in_specs=[smem(), anywhere()] + [vmem()] * 3,
        out_specs=(anywhere(), vmem()),
        scratch_shapes=[
            pltpu.VMEM((GROUPS, 6, ROWS, LANES), jnp.float32),
            pltpu.VMEM((VEL_LOCAL, 8, LANES), jnp.float32),
            pltpu.VMEM((16, LANES), jnp.float32),
            pltpu.VMEM((CHUNK, 48, LANES), jnp.float32),
            pltpu.SemaphoreType.DMA,
        ],
        input_output_aliases={1: 0},
        compiler_params=pltpu.CompilerParams(vmem_limit_bytes=16 * 2**20),
        name="enter_and_sum",
    )(place, kept, groups, f_edge, collision_rate)
    kept_near = lax.ppermute(kept, "gy", SWAP)
    total, kept_edge = sum_over_vert(partial, kept_edge)
    total_near = lax.ppermute(total, "gy", SWAP)
    total_edge = lax.ppermute(total[ROW_PACKED:], "gx", SWAP)
    own = tables_of(table_kernel, "xyz", "tables_own", total, collision_rate)
    near = tables_of(near_kernel, "y", "tables_near", total_near)
    moved_part = pl.pallas_call(
        second_inside_kernel,
        out_shape=f32(VEL_LOCAL, ROWS, LANES),
        in_specs=[smem(), vmem(), hbm()] + [vmem()] * 4,
        out_specs=vmem(),
        scratch_shapes=[
            pltpu.VMEM((VEL_LOCAL, ROWS, LANES), jnp.float32),
            pltpu.SemaphoreType.DMA((STEPS,)),
        ],
        compiler_params=pltpu.CompilerParams(vmem_limit_bytes=16 * 2**20),
        cost_estimate=pl.CostEstimate(flops=50000000, bytes_accessed=6000000, transcendentals=0),
        name="move_inside_two",
    )(place, kept, in_hbm(kept_near), *own[:2], *near[:2])
    return pl.pallas_call(
        second_kernel,
        out_shape=f32(VEL_LOCAL, ROWS, LANES),
        in_specs=[smem()] + [vmem()] * 8,
        out_specs=anywhere(),
        scratch_shapes=[
            pltpu.VMEM((8, LANES), jnp.float32),
            pltpu.VMEM((3, VG, 8, LANES), jnp.float32),
            pltpu.VMEM((2, 5, 8, LANES), jnp.float32),
            pltpu.VMEM((VG + 4, ROWS, LANES), jnp.float32),
            pltpu.VMEM((VEL_LOCAL, ROWS, LANES), jnp.float32),
            pltpu.VMEM((16, LANES), jnp.float32),
            pltpu.VMEM((CHUNK, 48, LANES), jnp.float32),
            pltpu.SemaphoreType.DMA((STEPS,)),
        ],
        compiler_params=pltpu.CompilerParams(vmem_limit_bytes=24 * 2**20),
        name="collide_two",
    )(
        place, moved_part, kept_edge, total, total_near, total_edge, collision_rate, own[2],
        near[2],
    )


def solution(mesh):
    split = Mesh(mesh.devices.reshape(2, 2, 4, 2, 8), ("gx", "gy", "x", "yl", "z"))
    placed = (P(VERT, "gx", "gy"), P("gx", "gy"))
    return jax.shard_map(
        body, mesh=split, in_specs=placed, out_specs=P(VERT, "gx", "gy"), check_vma=False
    )
```

```python
import functools
import math

import jax
import jax.numpy as jnp
from jax import lax
from jax.experimental import pallas as pl
from jax.experimental.pallas import tpu as pltpu
from jax.sharding import Mesh
from jax.sharding import PartitionSpec as P

VG = 20
VEL_LOCAL = 125
CHUNK = 5
CHUNKS = VEL_LOCAL // CHUNK
STEPS = 5
STEP_CHUNKS = CHUNKS // STEPS
PIECE = VEL_LOCAL // STEPS
GROUPS = 7
ROWS = 32
LANES = 128

SPACING = 9.0 / VG
LOWEST = 4.5 * (1.0 / VG - 1.0)
DT = 0.3 / 4.5
WEIGHT = (9.0 / VG) ** 3 / (2.0 * math.pi) ** 1.5
SPEEDS = [LOWEST + SPACING * n for n in range(VG)]

VERT = ("x", "yl", "z")
PLANE = ("x", "yl")

ROW_SECOND = 5 * ROWS
ROW_PACKED = 10 * ROWS
ROW_SPILL_X = 11 * ROWS
ROW_EDGE = ROW_SPILL_X + 20
ROW_COUNT = 12 * ROWS
HALF = LANES // 2
HALF_AT = 48
FEW = 12


def speed_of(index):
    return index.astype(jnp.float32) * SPACING + LOWEST


def lane_index():
    return lax.broadcasted_iota(jnp.int32, (ROWS, LANES), 1)


def other_plane(tile, even):
    return jnp.where(even, pltpu.roll(tile, LANES - 1, 1), pltpu.roll(tile, 1, 1))


def chunk_place(first, chunk):
    slot = lax.rem(first, VG) + chunk * CHUNK
    group = lax.div(slot, VG)
    whole = lax.div(first, VG) + group
    index_x = lax.div(whole, VG)
    return group, index_x, whole - index_x * VG, slot - group * VG


def y_sides(positive):
    lane = lane_index()
    if positive is True:
        return 2, 4, lane >= LANES - 2, lane >= LANES - 4
    if positive is False:
        return LANES - 2, LANES - 4, lane < 2, lane < 4
    one = ((lane + jnp.where(positive, 2, 0)) & (LANES - 1)) < 2
    two = ((lane + jnp.where(positive, 4, 0)) & (LANES - 1)) < 4
    return jnp.where(positive, 2, LANES - 2), jnp.where(positive, 4, LANES - 4), one, two


def y_part(center, near, sides):
    shift_one, shift_two, one, two = sides
    return pltpu.roll(jnp.where(one, near, center), shift_one, 1) - 0.25 * pltpu.roll(
        jnp.where(two, near, center), shift_two, 1
    )


def upwind(center, back, x_one, x_two, even, coef_x, coef_y, coef_z):
    return (
        center * (1.0 - 1.5 * (coef_x + coef_y) - 2.0 * coef_z)
        + (2.0 * coef_x) * (x_one - 0.25 * x_two)
        + (2.0 * coef_y) * back
        + (2.0 * coef_z) * other_plane(center, even)
    )


def each_sign(positive, run):
    for value in (True, False):
        pl.when(positive if value else jnp.logical_not(positive))(functools.partial(run, value))


def x_steps(buf, slot, center, halo, forward):
    buf[slot, 8:40] = center
    if forward:
        buf[slot, 6:8] = halo
        return buf[slot, 7:39], buf[slot, 6:38]
    buf[slot, 40:42] = halo
    return buf[slot, 9:41], buf[slot, 10:42]


def load_piece(f, held, sem, piece):
    rows = pl.ds(piece * PIECE, PIECE)
    return pltpu.make_async_copy(f.at[rows], held.at[rows], sem.at[piece])


def x_inside(center, forward):
    row = lax.broadcasted_iota(jnp.int32, (ROWS, LANES), 0)
    if forward:
        return [jnp.where(row >= n, pltpu.roll(center, n, 0), 0.0) for n in (1, 2)]
    return [jnp.where(row < ROWS - n, pltpu.roll(center, ROWS - n, 0), 0.0) for n in (1, 2)]


def send_kernel(place, f, out, band, sem):
    def take(forward):
        copy = pltpu.make_async_copy(f.at[:, pl.ds(24 if forward else 0, 8)], band, sem)
        copy.start()
        copy.wait()
        out[...] = band[:, 6:8] if forward else band[:, 0:2]

    each_sign(place[0] >= 32, take)


def hold_kernel(f, after, held, sem):
    del after
    copy = pltpu.make_async_copy(f, held, sem)
    copy.start()
    copy.wait()


def inside_kernel(
    place, held, f_near, rate, kept, kept_edge, groups, held_near, held_rate, sem_near, sem_rate
):
    rate_copy = pltpu.make_async_copy(rate, held_rate, sem_rate)
    rate_copy.start()
    for piece in range(STEPS):
        load_piece(f_near, held_near, sem_near, piece).start()
    rate_copy.wait()
    device = place[0]
    first = device * VEL_LOCAL
    even = lax.rem(lane_index(), 2) == 0
    keep = 1.0 - held_rate[...]
    groups[...] = jnp.zeros_like(groups)

    def move(forward):
        def chunk(c, carry):
            group, index_x, index_y, index_z = chunk_place(first, c)
            coef_x = DT * jnp.abs(speed_of(index_x))
            coef_y = DT * jnp.abs(speed_of(index_y))
            side = jnp.where(index_z >= VG // 2, 1.0, -1.0)

            sides = y_sides(index_y >= VG // 2)
            acc = [None] * 4
            at = [c * CHUNK + t for t in range(CHUNK)]
            speeds = [speed_of(index_z + t) for t in range(CHUNK)]
            centers = [held[v] for v in at]
            nears = [held_near[v] for v in at]
            backs = [y_part(center, near, sides) for center, near in zip(centers, nears)]
            moved = [
                upwind(center, back, *x_inside(center, forward), even, coef_x, coef_y,
                       DT * speed * side)
                for center, back, speed in zip(centers, backs, speeds)
            ]
            for value, speed in zip(moved, speeds):
                power = value
                for k in range(4):
                    acc[k] = power if acc[k] is None else acc[k] + power
                    if k < 3:
                        power = power * speed
            for v, value in zip(at, moved):
                left = keep * value
                kept[v] = left
                kept_edge[v] = left[30:32] if forward else left[0:2]
            for k in range(3):
                groups[group, k] += acc[k]
                groups[group, 3 + k] += side * acc[k + 1]

            return carry

        def piece(p, carry):
            load_piece(f_near, held_near, sem_near, p).wait()
            for c in range(STEP_CHUNKS):
                chunk(p * STEP_CHUNKS + c, carry)
            return carry

        lax.fori_loop(0, STEPS, piece, 0)

    each_sign(device >= 32, move)


def edge_kernel(
    place, kept_in, groups_in, f_edge, rate, kept, sums, groups, edge, few, buf, sem
):
    del kept_in
    device = place[0]
    first = device * VEL_LOCAL
    groups[...] = groups_in[...]
    even = lax.rem(lane_index(), 2) == 0
    keep = 1.0 - rate[...]

    def enter(forward):
        rows = slice(0, 2) if forward else slice(30, 32)
        inner = slice(0, 2) if forward else slice(6, 8)
        none = jnp.zeros((1, LANES), jnp.float32)
        band = kept.at[:, pl.ds(0 if forward else 24, 8)]
        load = pltpu.make_async_copy(band, edge, sem)
        load.start()
        load.wait()

        def chunk(c, carry):
            group, index_x, _, index_z = chunk_place(first, c)
            coef = (2.0 * DT) * jnp.abs(speed_of(index_x))
            side = jnp.where(index_z >= VG // 2, 1.0, -1.0)
            acc = [None] * 4
            for t in range(CHUNK):
                v = c * CHUNK + t
                halo = f_edge[v]
                one = [halo[1:2], none] if forward else [none, halo[0:1]]
                power = coef * (jnp.concatenate(one, axis=0) - 0.25 * halo)
                edge[v, inner] += keep[rows] * power
                speed_z = speed_of(index_z + t)
                for k in range(4):
                    acc[k] = power if acc[k] is None else acc[k] + power
                    if k < 3:
                        power = power * speed_z
            for k in range(3):
                groups[group, k, rows] += acc[k]
                groups[group, 3 + k, rows] += side * acc[k + 1]
            return carry

        def some(p, carry):
            for c in range(STEP_CHUNKS):
                chunk(p * STEP_CHUNKS + c, carry)
            return carry

        lax.fori_loop(0, STEPS, some, 0)
        store = pltpu.make_async_copy(edge, band, sem)
        store.start()
        return store

    def spread(forward):
        def one(group, carry):
            whole = lax.div(first, VG) + group
            index_x = lax.div(whole, VG)
            index_y = whole - index_x * VG
            speed_x = speed_of(index_x)
            speed_y = speed_of(index_y)
            coef_x = DT * jnp.abs(speed_x)
            coef_y = DT * jnp.abs(speed_y)
            squares = speed_x * speed_x + speed_y * speed_y

            def five(parts):
                return (
                    parts[0],
                    speed_x * parts[0],
                    speed_y * parts[0],
                    parts[1],
                    squares * parts[0] + parts[2],
                )

            sides = y_sides(index_y >= VG // 2)
            level = [WEIGHT * groups[group, k] for k in range(6)]
            for m, value in enumerate(five(level)):
                sums[ROWS * m : ROWS * (m + 1)] += value
            second, near_y, near_x = [], [], []
            for k in range(3):
                center = keep * level[k]
                absolute = keep * level[3 + k]
                x_one, x_two = x_steps(
                    buf, k, center, jnp.zeros((2, LANES), jnp.float32), forward
                )
                second.append(
                    center * (1.0 - 1.5 * (coef_x + coef_y))
                    - (2.0 * DT) * (absolute - other_plane(absolute, even))
                    + (2.0 * coef_x) * (x_one - 0.25 * x_two)
                    + (2.0 * coef_y) * y_part(center, 0.0, sides)
                )
                near_y.append(coef_y * jnp.where(sides[3], center, 0.0))
                near_x.append(coef_x * (center[30:32] if forward else center[0:2]))
            for m, value in enumerate(five(second)):
                sums[ROW_SECOND + ROWS * m : ROW_SECOND + ROWS * (m + 1)] += value
            for m, value in enumerate(five(near_x)):
                at = ROW_SPILL_X + 4 * m + (0 if forward else 2)
                sums[at : at + 2] += value
            packed = sums[ROW_PACKED : ROW_PACKED + ROWS]
            for m, value in enumerate(five(near_y)):
                packed = packed + (pltpu.roll(value, 8 * m, 1) if m else value)
            sums[ROW_PACKED : ROW_PACKED + ROWS] = packed

            return carry

        lax.fori_loop(0, GROUPS, one, 0)

    sums[...] = jnp.zeros_like(sums)

    def both(forward):
        store = enter(forward)
        spread(forward)
        store.wait()

    each_sign(device >= 32, both)
    for m in range(5):
        target, at = (sums, ROW_EDGE + 4 * m) if m < 3 else (few, 4 * (m - 3))
        target[at : at + 2] = sums[ROWS * m + 30 : ROWS * m + 32]
        target[at + 2 : at + 4] = sums[ROWS * m : ROWS * m + 2]
    few[8:16] = jnp.zeros((8, LANES), jnp.float32)

    @pl.when(device == 0)
    def _():
        few[8:10] = rate[30:32]
        few[10:12] = rate[0:2]
        lane = lane_index()
        border = jnp.where((lane < 4) | (lane >= LANES - 4), rate[...], 0.0)
        sums[ROW_PACKED : ROW_PACKED + ROWS] += pltpu.roll(border, 40, 1)

    rest = few[...]
    lane = lax.broadcasted_iota(jnp.int32, rest.shape, 1)
    left = pltpu.roll(jnp.where(lane < HALF, rest, 0.0), HALF_AT, 1)
    right = pltpu.roll(jnp.where(lane >= HALF, rest, 0.0), LANES - (HALF - HALF_AT), 1)
    sums[ROW_PACKED : ROW_PACKED + FEW] += left[0:FEW]
    sums[ROW_PACKED + FEW : ROW_PACKED + 2 * FEW] += right[0:FEW]


def parameters(moments):
    density = moments[0]
    share = 1.0 / density
    flow_x = moments[1] * share
    flow_y = moments[2] * share
    flow_z = moments[3] * share
    temper = (moments[4] * share - (flow_x * flow_x + flow_y * flow_y + flow_z * flow_z)) / 3.0
    return density / (temper * jnp.sqrt(temper)), flow_x, flow_y, flow_z, 0.5 / temper


def products(part_x, part_y, part_z):
    yz = part_y[0] * part_z[0]
    return (
        part_x[0] * yz,
        part_x[1] * yz,
        part_x[0] * (part_y[1] * part_z[0]),
        part_x[0] * (part_y[0] * part_z[1]),
        part_x[2] * yz + part_x[0] * (part_y[2] * part_z[0] + part_y[0] * part_z[2]),
    )


def one_block(at, moments, rate, base, tables, kinds, wanted):
    amp, flow_x, flow_y, flow_z, inv = parameters(moments)
    scale = amp * rate
    base[at] = scale
    full, plus, minus = [], [], []
    for d, flow in enumerate((flow_x, flow_y, flow_z)):
        halves = []
        for half in range(2):
            level = [None] * 4
            for n in range(half * 10, half * 10 + 10):
                gap = SPEEDS[n] - flow
                value = jnp.exp(-(inv * gap * gap))
                tables[d, n, at] = value
                for k in range(4):
                    term = value if k == 0 else value * (SPEEDS[n] ** k)
                    level[k] = term if level[k] is None else level[k] + term
            halves.append(level)
        full.append([halves[0][k] + halves[1][k] for k in range(3)])
        plus.append([halves[1][k + 1] for k in range(3)])
        minus.append([-halves[0][k + 1] for k in range(3)])
    scale = scale * WEIGHT
    x, y, z = [scale * part for part in full[0]], full[1], full[2]
    sets = {}
    if "x" in wanted:
        sets[0] = products([scale * part for part in plus[0]], y, z)
        sets[1] = products([scale * part for part in minus[0]], y, z)
    if "y" in wanted:
        sets[2] = products(x, plus[1], z)
        sets[3] = products(x, minus[1], z)
    if "z" in wanted:
        sets[4] = products(x, y, [plus[2][k] + minus[2][k] for k in range(3)])
        whole = products(x, y, z)
        sets[5] = [
            whole[m]
            - (1.5 * DT) * ((sets[0][m] + sets[1][m]) + (sets[2][m] + sets[3][m]))
            - (2.0 * DT) * sets[4][m]
            for m in range(5)
        ]
    for s, values in sets.items():
        for m in range(5):
            kinds[s, m, at] = values[m]


def table_kernel(wanted, total, rate, base, tables, kinds):
    for at in range(0, ROWS, 8):
        rows = slice(at, at + 8)
        one_block(
            rows, [total[ROWS * m + at : ROWS * m + at + 8] for m in range(5)], rate[rows], base,
            tables, kinds, wanted,
        )


def near_kernel(wanted, total, base, tables, kinds):
    for at in range(0, ROWS, 8):
        rate = pltpu.roll(total[ROW_PACKED + at : ROW_PACKED + at + 8], LANES - 40, 1)
        one_block(
            slice(at, at + 8), [total[ROWS * m + at : ROWS * m + at + 8] for m in range(5)], rate,
            base, tables, kinds, wanted,
        )


def second_inside_kernel(
    place, kept, kept_near, base, tables, base_near, tables_near, moved_part, held_near, sem
):
    for piece in range(STEPS):
        load_piece(kept_near, held_near, sem, piece).start()
    device = place[0]
    first = device * VEL_LOCAL
    even = lax.rem(lane_index(), 2) == 0

    def move(forward):
        def chunk(c, carry):
            group, index_x, index_y, index_z = chunk_place(first, c)
            coef_x = DT * jnp.abs(speed_of(index_x))
            coef_y = DT * jnp.abs(speed_of(index_y))
            side = jnp.where(index_z >= VG // 2, 1.0, -1.0)
            sides = y_sides(index_y >= VG // 2)
            front = base[...] * tables[0, index_x] * tables[1, index_y]
            front_near = base_near[...] * tables_near[0, index_x] * tables_near[1, index_y]
            at = [c * CHUNK + t for t in range(CHUNK)]
            centers = [kept[v] + front * tables[2, index_z + t] for t, v in enumerate(at)]
            nears = [
                held_near[v] + front_near * tables_near[2, index_z + t] for t, v in enumerate(at)
            ]
            backs = [y_part(center, near, sides) for center, near in zip(centers, nears)]
            for t, v in enumerate(at):
                moved_part[v] = upwind(
                    centers[t], backs[t], *x_inside(centers[t], forward), even, coef_x, coef_y,
                    DT * speed_of(index_z + t) * side,
                )
            return carry

        def piece(p, carry):
            load_piece(kept_near, held_near, sem, p).wait()
            for c in range(STEP_CHUNKS):
                chunk(p * STEP_CHUNKS + c, carry)
            return carry

        lax.fori_loop(0, STEPS, piece, 0)

    each_sign(device >= 32, move)


def second_kernel(
    place, moved_part, kept_edge, total, total_near, total_edge, rate, kinds, kinds_near,
    out, base_edge, tables_edge, kinds_edge, table_two, done, few, buf, sem,
):
    device = place[0]
    first = device * VEL_LOCAL
    even = lax.rem(lane_index(), 2) == 0
    keep = 1.0 - rate[...]

    left = pltpu.roll(total_edge[0:16], LANES - HALF_AT, 1)
    right = pltpu.roll(total_edge[FEW : FEW + 16], HALF - HALF_AT, 1)
    few[...] = jnp.where(lax.broadcasted_iota(jnp.int32, left.shape, 1) < HALF, left, right)

    def edge(source, row):
        rows = source[row : row + 4]
        return jnp.concatenate([rows, rows], axis=0)

    one_block(
        slice(0, 8),
        [edge(total_edge, ROWS + 20 + 4 * m) for m in range(3)] + [edge(few, 0), edge(few, 4)],
        edge(few, 8), base_edge,
        tables_edge, kinds_edge, "x",
    )
    spill_y = total_near[ROW_PACKED : ROW_PACKED + ROWS]
    moments = []
    for m in range(5):
        result = total[ROW_SECOND + ROWS * m : ROW_SECOND + ROWS * (m + 1)] + kinds[5, m]
        x_one, x_two = x_steps(
            buf, 0, kinds[0, m],
            kinds_edge[0, m, 0:2] + (1.0 / DT) * total_edge[ROWS + 4 * m : ROWS + 4 * m + 2], True,
        )
        x_low, x_lower = x_steps(
            buf, 1, kinds[1, m],
            kinds_edge[1, m, 2:4] + (1.0 / DT) * total_edge[ROWS + 4 * m + 2 : ROWS + 4 * m + 4], False,
        )
        spill = pltpu.roll(spill_y, LANES - 8 * m, 1) if m else spill_y
        spill = (1.0 / DT) * spill
        moments.append(
            result
            + (2.0 * DT)
            * (
                other_plane(kinds[4, m], even)
                + (x_one - 0.25 * x_two)
                + (x_low - 0.25 * x_lower)
                + y_part(kinds[2, m], kinds_near[2, m] + spill, y_sides(True))
                + y_part(kinds[3, m], kinds_near[3, m] + spill, y_sides(False))
            )
        )
    amp, flow_x, flow_y, flow_z, inv = parameters(moments)
    for n in range(VG):
        gap = SPEEDS[n] - flow_z
        table_two[n] = jnp.exp(-(inv * gap * gap))
    table_two[VG] = amp * rate[...]
    table_two[VG + 1] = flow_x
    table_two[VG + 2] = flow_y
    table_two[VG + 3] = inv


    def move(forward):
        row = 0 if forward else 2
        rows = slice(0, 2) if forward else slice(30, 32)
        none = jnp.zeros((1, LANES), jnp.float32)

        def chunk(c, carry):
            group, index_x, index_y, index_z = chunk_place(first, c)
            speed_x = speed_of(index_x)
            coef = (2.0 * DT) * jnp.abs(speed_x)
            gap_x = speed_x - table_two[VG + 1]
            gap_y = speed_of(index_y) - table_two[VG + 2]
            front_two = table_two[VG] * jnp.exp(
                -(table_two[VG + 3] * (gap_x * gap_x + gap_y * gap_y))
            )
            front_edge = base_edge[...] * tables_edge[0, index_x] * tables_edge[1, index_y]
            for t in range(CHUNK):
                v = c * CHUNK + t
                n = index_z + t
                halo = kept_edge[v] + (front_edge * tables_edge[2, n])[row : row + 2]
                one = [halo[1:2], none] if forward else [none, halo[0:1]]
                entered = coef * (jnp.concatenate(one, axis=0) - 0.25 * halo)
                done[v] = keep * moved_part[v] + front_two * table_two[n]
                done[v, rows] += keep[rows] * entered
            return carry

        def piece(p, carry):
            for c in range(STEP_CHUNKS):
                chunk(p * STEP_CHUNKS + c, carry)
            load_piece(done, out, sem, p).start()
            return carry

        lax.fori_loop(0, STEPS, piece, 0)

    each_sign(device >= 32, move)
    for piece in range(STEPS):
        load_piece(done, out, sem, piece).wait()


def vmem():
    return pl.BlockSpec(memory_space=pltpu.VMEM)


def in_hbm(x):
    return pltpu.with_memory_space_constraint(x, pltpu.HBM)


def hbm():
    return pl.BlockSpec(memory_space=pltpu.HBM)


def anywhere():
    return pl.BlockSpec(memory_space=pl.ANY)


def smem():
    return pl.BlockSpec(memory_space=pltpu.SMEM)


SWAP = [(0, 1), (1, 0)]


def sum_over_vert(partial, beside):
    parts = partial.reshape(8, -1, 8, LANES)
    share = jnp.sum(lax.all_to_all(parts, PLANE, 0, 0), axis=0)
    share = jnp.sum(lax.all_to_all(jnp.broadcast_to(share[None], parts.shape), "z", 0, 0), axis=0)
    share, beside = lax.optimization_barrier((share, beside))
    whole = lax.all_to_all(jnp.broadcast_to(share[None], parts.shape), PLANE, 0, 0)
    return whole.reshape(ROW_COUNT, LANES), beside


def f32(*shape):
    return jax.ShapeDtypeStruct(shape, jnp.float32)


def tables_of(kernel, wanted, name, *operands):
    return pl.pallas_call(
        functools.partial(kernel, wanted),
        out_shape=(
            f32(ROWS, LANES), f32(3, VG, ROWS, LANES), f32(6, 5, ROWS, LANES)
        ),
        in_specs=[vmem()] * len(operands),
        out_specs=(vmem(), vmem(), vmem()),
        compiler_params=pltpu.CompilerParams(vmem_limit_bytes=16 * 2**20),
        cost_estimate=pl.CostEstimate(flops=8000000, bytes_accessed=3000000, transcendentals=250000),
        name=name,
    )(*operands)


def body(distribution, collision_rate):
    device = lax.axis_index(VERT)
    place = device.astype(jnp.int32).reshape(1)
    rows = pl.pallas_call(
        send_kernel,
        out_shape=f32(VEL_LOCAL, 2, LANES),
        in_specs=[smem(), hbm()],
        out_specs=vmem(),
        scratch_shapes=[pltpu.VMEM((VEL_LOCAL, 8, LANES), jnp.float32), pltpu.SemaphoreType.DMA],
        compiler_params=pltpu.CompilerParams(vmem_limit_bytes=24 * 2**20),
        cost_estimate=pl.CostEstimate(flops=0, bytes_accessed=600000, transcendentals=0),
        name="send_rows",
    )(place, in_hbm(distribution))
    f_edge = lax.ppermute(rows, "gx", SWAP)
    held = pl.pallas_call(
        hold_kernel,
        out_shape=f32(VEL_LOCAL, ROWS, LANES),
        in_specs=[hbm(), anywhere()],
        out_specs=vmem(),
        scratch_shapes=[pltpu.SemaphoreType.DMA],
        compiler_params=pltpu.CompilerParams(vmem_limit_bytes=16 * 2**20),
        cost_estimate=pl.CostEstimate(flops=0, bytes_accessed=4000000, transcendentals=0),
        name="hold",
    )(in_hbm(distribution), rows)
    f_near = lax.ppermute(distribution, "gy", SWAP)
    kept, kept_edge, groups = pl.pallas_call(
        inside_kernel,
        out_shape=(
            f32(VEL_LOCAL, ROWS, LANES), f32(VEL_LOCAL, 2, LANES), f32(GROUPS, 6, ROWS, LANES)
        ),
        in_specs=[smem(), vmem(), hbm(), hbm()],
        out_specs=(vmem(), vmem(), vmem()),
        scratch_shapes=[
            pltpu.VMEM((VEL_LOCAL, ROWS, LANES), jnp.float32),
            pltpu.VMEM((ROWS, LANES), jnp.float32),
            pltpu.SemaphoreType.DMA((STEPS,)),
            pltpu.SemaphoreType.DMA,
        ],
        compiler_params=pltpu.CompilerParams(vmem_limit_bytes=16 * 2**20),
        cost_estimate=pl.CostEstimate(flops=50000000, bytes_accessed=6000000, transcendentals=0),
        name="move_inside",
    )(place, held, in_hbm(f_near), in_hbm(collision_rate))
    kept_edge = lax.ppermute(kept_edge, "gx", SWAP)
    kept, partial = pl.pallas_call(
        edge_kernel,
        out_shape=(f32(VEL_LOCAL, ROWS, LANES), f32(ROW_COUNT, LANES)),
        in_specs=[smem(), anywhere()] + [vmem()] * 3,
        out_specs=(anywhere(), vmem()),
        scratch_shapes=[
            pltpu.VMEM((GROUPS, 6, ROWS, LANES), jnp.float32),
            pltpu.VMEM((VEL_LOCAL, 8, LANES), jnp.float32),
            pltpu.VMEM((16, LANES), jnp.float32),
            pltpu.VMEM((CHUNK, 48, LANES), jnp.float32),
            pltpu.SemaphoreType.DMA,
        ],
        input_output_aliases={1: 0},
        compiler_params=pltpu.CompilerParams(vmem_limit_bytes=16 * 2**20),
        name="enter_and_sum",
    )(place, kept, groups, f_edge, collision_rate)
    kept_near = lax.ppermute(kept, "gy", SWAP)
    total, kept_edge = sum_over_vert(partial, kept_edge)
    total_near = lax.ppermute(total, "gy", SWAP)
    total_edge = lax.ppermute(total[ROW_PACKED:], "gx", SWAP)
    own = tables_of(table_kernel, "xyz", "tables_own", total, collision_rate)
    near = tables_of(near_kernel, "y", "tables_near", total_near)
    moved_part = pl.pallas_call(
        second_inside_kernel,
        out_shape=f32(VEL_LOCAL, ROWS, LANES),
        in_specs=[smem(), vmem(), hbm()] + [vmem()] * 4,
        out_specs=vmem(),
        scratch_shapes=[
            pltpu.VMEM((VEL_LOCAL, ROWS, LANES), jnp.float32),
            pltpu.SemaphoreType.DMA((STEPS,)),
        ],
        compiler_params=pltpu.CompilerParams(vmem_limit_bytes=16 * 2**20),
        cost_estimate=pl.CostEstimate(flops=50000000, bytes_accessed=6000000, transcendentals=0),
        name="move_inside_two",
    )(place, kept, in_hbm(kept_near), *own[:2], *near[:2])
    return pl.pallas_call(
        second_kernel,
        out_shape=f32(VEL_LOCAL, ROWS, LANES),
        in_specs=[smem()] + [vmem()] * 8,
        out_specs=anywhere(),
        scratch_shapes=[
            pltpu.VMEM((8, LANES), jnp.float32),
            pltpu.VMEM((3, VG, 8, LANES), jnp.float32),
            pltpu.VMEM((2, 5, 8, LANES), jnp.float32),
            pltpu.VMEM((VG + 4, ROWS, LANES), jnp.float32),
            pltpu.VMEM((VEL_LOCAL, ROWS, LANES), jnp.float32),
            pltpu.VMEM((16, LANES), jnp.float32),
            pltpu.VMEM((CHUNK, 48, LANES), jnp.float32),
            pltpu.SemaphoreType.DMA((STEPS,)),
        ],
        compiler_params=pltpu.CompilerParams(vmem_limit_bytes=24 * 2**20),
        name="collide_two",
    )(
        place, moved_part, kept_edge, total, total_near, total_edge, collision_rate, own[2],
        near[2],
    )


def solution(mesh):
    split = Mesh(mesh.devices.reshape(2, 2, 4, 2, 8), ("gx", "gy", "x", "yl", "z"))
    placed = (P(VERT, "gx", "gy"), P("gx", "gy"))
    return jax.shard_map(
        body, mesh=split, in_specs=placed, out_specs=P(VERT, "gx", "gy"), check_vma=False
    )
```

```python
import functools
import math

import jax
import jax.numpy as jnp
from jax import lax
from jax.experimental import pallas as pl
from jax.experimental.pallas import tpu as pltpu
from jax.sharding import Mesh
from jax.sharding import PartitionSpec as P

VG = 20
VEL_LOCAL = 125
CHUNK = 5
CHUNKS = VEL_LOCAL // CHUNK
STEPS = 5
STEP_CHUNKS = CHUNKS // STEPS
PIECE = VEL_LOCAL // STEPS
GROUPS = 7
ROWS = 32
LANES = 128

SPACING = 9.0 / VG
LOWEST = 4.5 * (1.0 / VG - 1.0)
DT = 0.3 / 4.5
WEIGHT = (9.0 / VG) ** 3 / (2.0 * math.pi) ** 1.5
SPEEDS = [LOWEST + SPACING * n for n in range(VG)]

VERT = ("x", "yl", "z")
PLANE = ("x", "yl")

ROW_SECOND = 5 * ROWS
ROW_PACKED = 10 * ROWS
ROW_SPILL_X = 11 * ROWS
ROW_EDGE = ROW_SPILL_X + 20
ROW_COUNT = 12 * ROWS
HALF = LANES // 2
HALF_AT = 48
FEW = 12


def speed_of(index):
    return index.astype(jnp.float32) * SPACING + LOWEST


def lane_index():
    return lax.broadcasted_iota(jnp.int32, (ROWS, LANES), 1)


def other_plane(tile, even):
    return jnp.where(even, pltpu.roll(tile, LANES - 1, 1), pltpu.roll(tile, 1, 1))


def chunk_place(first, chunk):
    slot = lax.rem(first, VG) + chunk * CHUNK
    group = lax.div(slot, VG)
    whole = lax.div(first, VG) + group
    index_x = lax.div(whole, VG)
    return group, index_x, whole - index_x * VG, slot - group * VG


def y_sides(positive):
    lane = lane_index()
    if positive is True:
        return 2, 4, lane >= LANES - 2, lane >= LANES - 4
    if positive is False:
        return LANES - 2, LANES - 4, lane < 2, lane < 4
    one = ((lane + jnp.where(positive, 2, 0)) & (LANES - 1)) < 2
    two = ((lane + jnp.where(positive, 4, 0)) & (LANES - 1)) < 4
    return jnp.where(positive, 2, LANES - 2), jnp.where(positive, 4, LANES - 4), one, two


def y_part(center, near, sides):
    shift_one, shift_two, one, two = sides
    return pltpu.roll(jnp.where(one, near, center), shift_one, 1) - 0.25 * pltpu.roll(
        jnp.where(two, near, center), shift_two, 1
    )


def upwind(center, back, x_one, x_two, even, coef_x, coef_y, coef_z):
    return (
        center * (1.0 - 1.5 * (coef_x + coef_y) - 2.0 * coef_z)
        + (2.0 * coef_x) * (x_one - 0.25 * x_two)
        + (2.0 * coef_y) * back
        + (2.0 * coef_z) * other_plane(center, even)
    )


def each_sign(positive, run):
    for value in (True, False):
        pl.when(positive if value else jnp.logical_not(positive))(functools.partial(run, value))


def x_steps(buf, slot, center, halo, forward):
    buf[slot, 8:40] = center
    if forward:
        buf[slot, 6:8] = halo
        return buf[slot, 7:39], buf[slot, 6:38]
    buf[slot, 40:42] = halo
    return buf[slot, 9:41], buf[slot, 10:42]


def load_piece(f, held, sem, piece):
    rows = pl.ds(piece * PIECE, PIECE)
    return pltpu.make_async_copy(f.at[rows], held.at[rows], sem.at[piece])


def x_inside(center, forward):
    row = lax.broadcasted_iota(jnp.int32, (ROWS, LANES), 0)
    if forward:
        return [jnp.where(row >= n, pltpu.roll(center, n, 0), 0.0) for n in (1, 2)]
    return [jnp.where(row < ROWS - n, pltpu.roll(center, ROWS - n, 0), 0.0) for n in (1, 2)]


def send_kernel(place, f, out, band, sem):
    def take(forward):
        copy = pltpu.make_async_copy(f.at[:, pl.ds(24 if forward else 0, 8)], band, sem)
        copy.start()
        copy.wait()
        out[...] = band[:, 6:8] if forward else band[:, 0:2]

    each_sign(place[0] >= 32, take)


def hold_kernel(f, after, held, sem):
    del after
    copy = pltpu.make_async_copy(f, held, sem)
    copy.start()
    copy.wait()


def inside_kernel(
    place, held, f_near, rate, kept, kept_edge, groups, held_near, held_rate, sem_near, sem_rate
):
    rate_copy = pltpu.make_async_copy(rate, held_rate, sem_rate)
    rate_copy.start()
    for piece in range(STEPS):
        load_piece(f_near, held_near, sem_near, piece).start()
    rate_copy.wait()
    device = place[0]
    first = device * VEL_LOCAL
    even = lax.rem(lane_index(), 2) == 0
    keep = 1.0 - held_rate[...]
    groups[...] = jnp.zeros_like(groups)

    def move(forward):
        def chunk(c, carry):
            group, index_x, index_y, index_z = chunk_place(first, c)
            coef_x = DT * jnp.abs(speed_of(index_x))
            coef_y = DT * jnp.abs(speed_of(index_y))
            side = jnp.where(index_z >= VG // 2, 1.0, -1.0)

            sides = y_sides(index_y >= VG // 2)
            acc = [None] * 4
            at = [c * CHUNK + t for t in range(CHUNK)]
            speeds = [speed_of(index_z + t) for t in range(CHUNK)]
            centers = [held[v] for v in at]
            nears = [held_near[v] for v in at]
            backs = [y_part(center, near, sides) for center, near in zip(centers, nears)]
            moved = [
                upwind(center, back, *x_inside(center, forward), even, coef_x, coef_y,
                       DT * speed * side)
                for center, back, speed in zip(centers, backs, speeds)
            ]
            for value, speed in zip(moved, speeds):
                power = value
                for k in range(4):
                    acc[k] = power if acc[k] is None else acc[k] + power
                    if k < 3:
                        power = power * speed
            for v, value in zip(at, moved):
                left = keep * value
                kept[v] = left
                kept_edge[v] = left[30:32] if forward else left[0:2]
            for k in range(3):
                groups[group, k] += acc[k]
                groups[group, 3 + k] += side * acc[k + 1]

            return carry

        def piece(p, carry):
            load_piece(f_near, held_near, sem_near, p).wait()
            for c in range(STEP_CHUNKS):
                chunk(p * STEP_CHUNKS + c, carry)
            return carry

        lax.fori_loop(0, STEPS, piece, 0)

    each_sign(device >= 32, move)


def edge_kernel(
    place, kept_in, groups_in, f_edge, rate, kept, sums, groups, edge, few, buf, sem
):
    del kept_in
    device = place[0]
    first = device * VEL_LOCAL
    even = lax.rem(lane_index(), 2) == 0
    keep = 1.0 - rate[...]

    def enter(forward):
        rows = slice(0, 2) if forward else slice(30, 32)
        inner = slice(0, 2) if forward else slice(6, 8)
        none = jnp.zeros((1, LANES), jnp.float32)
        band = kept.at[:, pl.ds(0 if forward else 24, 8)]
        load = pltpu.make_async_copy(band, edge, sem)
        load.start()
        groups[...] = groups_in[...]
        load.wait()

        def chunk(c, carry):
            group, index_x, _, index_z = chunk_place(first, c)
            coef = (2.0 * DT) * jnp.abs(speed_of(index_x))
            side = jnp.where(index_z >= VG // 2, 1.0, -1.0)
            acc = [None] * 4
            for t in range(CHUNK):
                v = c * CHUNK + t
                halo = f_edge[v]
                one = [halo[1:2], none] if forward else [none, halo[0:1]]
                power = coef * (jnp.concatenate(one, axis=0) - 0.25 * halo)
                edge[v, inner] += keep[rows] * power
                speed_z = speed_of(index_z + t)
                for k in range(4):
                    acc[k] = power if acc[k] is None else acc[k] + power
                    if k < 3:
                        power = power * speed_z
            for k in range(3):
                groups[group, k, rows] += acc[k]
                groups[group, 3 + k, rows] += side * acc[k + 1]
            return carry

        def some(p, carry):
            for c in range(STEP_CHUNKS):
                chunk(p * STEP_CHUNKS + c, carry)
            return carry

        lax.fori_loop(0, STEPS, some, 0)
        store = pltpu.make_async_copy(edge, band, sem)
        store.start()
        return store

    def spread(forward):
        def one(group, carry):
            whole = lax.div(first, VG) + group
            index_x = lax.div(whole, VG)
            index_y = whole - index_x * VG
            speed_x = speed_of(index_x)
            speed_y = speed_of(index_y)
            coef_x = DT * jnp.abs(speed_x)
            coef_y = DT * jnp.abs(speed_y)
            squares = speed_x * speed_x + speed_y * speed_y

            def five(parts):
                return (
                    parts[0],
                    speed_x * parts[0],
                    speed_y * parts[0],
                    parts[1],
                    squares * parts[0] + parts[2],
                )

            sides = y_sides(index_y >= VG // 2)
            level = [WEIGHT * groups[group, k] for k in range(6)]
            for m, value in enumerate(five(level)):
                sums[ROWS * m : ROWS * (m + 1)] += value
            second, near_y, near_x = [], [], []
            for k in range(3):
                center = keep * level[k]
                absolute = keep * level[3 + k]
                x_one, x_two = x_steps(
                    buf, k, center, jnp.zeros((2, LANES), jnp.float32), forward
                )
                second.append(
                    center * (1.0 - 1.5 * (coef_x + coef_y))
                    - (2.0 * DT) * (absolute - other_plane(absolute, even))
                    + (2.0 * coef_x) * (x_one - 0.25 * x_two)
                    + (2.0 * coef_y) * y_part(center, 0.0, sides)
                )
                near_y.append(coef_y * jnp.where(sides[3], center, 0.0))
                near_x.append(coef_x * (center[30:32] if forward else center[0:2]))
            for m, value in enumerate(five(second)):
                sums[ROW_SECOND + ROWS * m : ROW_SECOND + ROWS * (m + 1)] += value
            for m, value in enumerate(five(near_x)):
                at = ROW_SPILL_X + 4 * m + (0 if forward else 2)
                sums[at : at + 2] += value
            packed = sums[ROW_PACKED : ROW_PACKED + ROWS]
            for m, value in enumerate(five(near_y)):
                packed = packed + (pltpu.roll(value, 8 * m, 1) if m else value)
            sums[ROW_PACKED : ROW_PACKED + ROWS] = packed

            return carry

        lax.fori_loop(0, GROUPS, one, 0)

    sums[...] = jnp.zeros_like(sums)

    def both(forward):
        store = enter(forward)
        spread(forward)
        store.wait()

    each_sign(device >= 32, both)
    for m in range(5):
        target, at = (sums, ROW_EDGE + 4 * m) if m < 3 else (few, 4 * (m - 3))
        target[at : at + 2] = sums[ROWS * m + 30 : ROWS * m + 32]
        target[at + 2 : at + 4] = sums[ROWS * m : ROWS * m + 2]
    few[8:16] = jnp.zeros((8, LANES), jnp.float32)

    @pl.when(device == 0)
    def _():
        few[8:10] = rate[30:32]
        few[10:12] = rate[0:2]
        lane = lane_index()
        border = jnp.where((lane < 4) | (lane >= LANES - 4), rate[...], 0.0)
        sums[ROW_PACKED : ROW_PACKED + ROWS] += pltpu.roll(border, 40, 1)

    rest = few[...]
    lane = lax.broadcasted_iota(jnp.int32, rest.shape, 1)
    left = pltpu.roll(jnp.where(lane < HALF, rest, 0.0), HALF_AT, 1)
    right = pltpu.roll(jnp.where(lane >= HALF, rest, 0.0), LANES - (HALF - HALF_AT), 1)
    sums[ROW_PACKED : ROW_PACKED + FEW] += left[0:FEW]
    sums[ROW_PACKED + FEW : ROW_PACKED + 2 * FEW] += right[0:FEW]


def parameters(moments):
    density = moments[0]
    share = 1.0 / density
    flow_x = moments[1] * share
    flow_y = moments[2] * share
    flow_z = moments[3] * share
    temper = (moments[4] * share - (flow_x * flow_x + flow_y * flow_y + flow_z * flow_z)) / 3.0
    return density / (temper * jnp.sqrt(temper)), flow_x, flow_y, flow_z, 0.5 / temper


def products(part_x, part_y, part_z):
    yz = part_y[0] * part_z[0]
    return (
        part_x[0] * yz,
        part_x[1] * yz,
        part_x[0] * (part_y[1] * part_z[0]),
        part_x[0] * (part_y[0] * part_z[1]),
        part_x[2] * yz + part_x[0] * (part_y[2] * part_z[0] + part_y[0] * part_z[2]),
    )


def one_block(at, moments, rate, base, tables, kinds, wanted):
    amp, flow_x, flow_y, flow_z, inv = parameters(moments)
    scale = amp * rate
    base[at] = scale
    full, plus, minus = [], [], []
    for d, flow in enumerate((flow_x, flow_y, flow_z)):
        halves = []
        for half in range(2):
            level = [None] * 4
            for n in range(half * 10, half * 10 + 10):
                gap = SPEEDS[n] - flow
                value = jnp.exp(-(inv * gap * gap))
                tables[d, n, at] = value
                for k in range(4):
                    term = value if k == 0 else value * (SPEEDS[n] ** k)
                    level[k] = term if level[k] is None else level[k] + term
            halves.append(level)
        full.append([halves[0][k] + halves[1][k] for k in range(3)])
        plus.append([halves[1][k + 1] for k in range(3)])
        minus.append([-halves[0][k + 1] for k in range(3)])
    scale = scale * WEIGHT
    x, y, z = [scale * part for part in full[0]], full[1], full[2]
    sets = {}
    if "x" in wanted:
        sets[0] = products([scale * part for part in plus[0]], y, z)
        sets[1] = products([scale * part for part in minus[0]], y, z)
    if "y" in wanted:
        sets[2] = products(x, plus[1], z)
        sets[3] = products(x, minus[1], z)
    if "z" in wanted:
        sets[4] = products(x, y, [plus[2][k] + minus[2][k] for k in range(3)])
        whole = products(x, y, z)
        sets[5] = [
            whole[m]
            - (1.5 * DT) * ((sets[0][m] + sets[1][m]) + (sets[2][m] + sets[3][m]))
            - (2.0 * DT) * sets[4][m]
            for m in range(5)
        ]
    for s, values in sets.items():
        for m in range(5):
            kinds[s, m, at] = values[m]


def table_kernel(wanted, total, rate, base, tables, kinds):
    for at in range(0, ROWS, 8):
        rows = slice(at, at + 8)
        one_block(
            rows, [total[ROWS * m + at : ROWS * m + at + 8] for m in range(5)], rate[rows], base,
            tables, kinds, wanted,
        )


def near_kernel(wanted, total, base, tables, kinds):
    for at in range(0, ROWS, 8):
        rate = pltpu.roll(total[ROW_PACKED + at : ROW_PACKED + at + 8], LANES - 40, 1)
        one_block(
            slice(at, at + 8), [total[ROWS * m + at : ROWS * m + at + 8] for m in range(5)], rate,
            base, tables, kinds, wanted,
        )


def second_inside_kernel(
    place, kept, kept_near, base, tables, base_near, tables_near, moved_part, held_near, sem
):
    for piece in range(STEPS):
        load_piece(kept_near, held_near, sem, piece).start()
    device = place[0]
    first = device * VEL_LOCAL
    even = lax.rem(lane_index(), 2) == 0

    def move(forward):
        def chunk(c, carry):
            group, index_x, index_y, index_z = chunk_place(first, c)
            coef_x = DT * jnp.abs(speed_of(index_x))
            coef_y = DT * jnp.abs(speed_of(index_y))
            side = jnp.where(index_z >= VG // 2, 1.0, -1.0)
            sides = y_sides(index_y >= VG // 2)
            front = base[...] * tables[0, index_x] * tables[1, index_y]
            front_near = base_near[...] * tables_near[0, index_x] * tables_near[1, index_y]
            at = [c * CHUNK + t for t in range(CHUNK)]
            centers = [kept[v] + front * tables[2, index_z + t] for t, v in enumerate(at)]
            nears = [
                held_near[v] + front_near * tables_near[2, index_z + t] for t, v in enumerate(at)
            ]
            backs = [y_part(center, near, sides) for center, near in zip(centers, nears)]
            for t, v in enumerate(at):
                moved_part[v] = upwind(
                    centers[t], backs[t], *x_inside(centers[t], forward), even, coef_x, coef_y,
                    DT * speed_of(index_z + t) * side,
                )
            return carry

        def piece(p, carry):
            load_piece(kept_near, held_near, sem, p).wait()
            for c in range(STEP_CHUNKS):
                chunk(p * STEP_CHUNKS + c, carry)
            return carry

        lax.fori_loop(0, STEPS, piece, 0)

    each_sign(device >= 32, move)


def second_kernel(
    place, moved_part, kept_edge, total, total_near, total_edge, rate, kinds, kinds_near,
    out, base_edge, tables_edge, kinds_edge, table_two, done, few, buf, sem,
):
    device = place[0]
    first = device * VEL_LOCAL
    even = lax.rem(lane_index(), 2) == 0
    keep = 1.0 - rate[...]

    left = pltpu.roll(total_edge[0:16], LANES - HALF_AT, 1)
    right = pltpu.roll(total_edge[FEW : FEW + 16], HALF - HALF_AT, 1)
    few[...] = jnp.where(lax.broadcasted_iota(jnp.int32, left.shape, 1) < HALF, left, right)

    def edge(source, row):
        rows = source[row : row + 4]
        return jnp.concatenate([rows, rows], axis=0)

    one_block(
        slice(0, 8),
        [edge(total_edge, ROWS + 20 + 4 * m) for m in range(3)] + [edge(few, 0), edge(few, 4)],
        edge(few, 8), base_edge,
        tables_edge, kinds_edge, "x",
    )
    spill_y = total_near[ROW_PACKED : ROW_PACKED + ROWS]
    moments = []
    for m in range(5):
        result = total[ROW_SECOND + ROWS * m : ROW_SECOND + ROWS * (m + 1)] + kinds[5, m]
        x_one, x_two = x_steps(
            buf, 0, kinds[0, m],
            kinds_edge[0, m, 0:2] + (1.0 / DT) * total_edge[ROWS + 4 * m : ROWS + 4 * m + 2], True,
        )
        x_low, x_lower = x_steps(
            buf, 1, kinds[1, m],
            kinds_edge[1, m, 2:4] + (1.0 / DT) * total_edge[ROWS + 4 * m + 2 : ROWS + 4 * m + 4], False,
        )
        spill = pltpu.roll(spill_y, LANES - 8 * m, 1) if m else spill_y
        spill = (1.0 / DT) * spill
        moments.append(
            result
            + (2.0 * DT)
            * (
                other_plane(kinds[4, m], even)
                + (x_one - 0.25 * x_two)
                + (x_low - 0.25 * x_lower)
                + y_part(kinds[2, m], kinds_near[2, m] + spill, y_sides(True))
                + y_part(kinds[3, m], kinds_near[3, m] + spill, y_sides(False))
            )
        )
    amp, flow_x, flow_y, flow_z, inv = parameters(moments)
    for n in range(VG):
        gap = SPEEDS[n] - flow_z
        table_two[n] = jnp.exp(-(inv * gap * gap))
    table_two[VG] = amp * rate[...]
    table_two[VG + 1] = flow_x
    table_two[VG + 2] = flow_y
    table_two[VG + 3] = inv


    def move(forward):
        row = 0 if forward else 2
        rows = slice(0, 2) if forward else slice(30, 32)
        none = jnp.zeros((1, LANES), jnp.float32)

        def chunk(c, carry):
            group, index_x, index_y, index_z = chunk_place(first, c)
            speed_x = speed_of(index_x)
            coef = (2.0 * DT) * jnp.abs(speed_x)
            gap_x = speed_x - table_two[VG + 1]
            gap_y = speed_of(index_y) - table_two[VG + 2]
            front_two = table_two[VG] * jnp.exp(
                -(table_two[VG + 3] * (gap_x * gap_x + gap_y * gap_y))
            )
            front_edge = base_edge[...] * tables_edge[0, index_x] * tables_edge[1, index_y]
            for t in range(CHUNK):
                v = c * CHUNK + t
                n = index_z + t
                halo = kept_edge[v] + (front_edge * tables_edge[2, n])[row : row + 2]
                one = [halo[1:2], none] if forward else [none, halo[0:1]]
                entered = coef * (jnp.concatenate(one, axis=0) - 0.25 * halo)
                done[v] = keep * moved_part[v] + front_two * table_two[n]
                done[v, rows] += keep[rows] * entered
            return carry

        def piece(p, carry):
            for c in range(STEP_CHUNKS):
                chunk(p * STEP_CHUNKS + c, carry)
            load_piece(done, out, sem, p).start()
            return carry

        lax.fori_loop(0, STEPS, piece, 0)

    each_sign(device >= 32, move)
    for piece in range(STEPS):
        load_piece(done, out, sem, piece).wait()


def vmem():
    return pl.BlockSpec(memory_space=pltpu.VMEM)


def in_hbm(x):
    return pltpu.with_memory_space_constraint(x, pltpu.HBM)


def hbm():
    return pl.BlockSpec(memory_space=pltpu.HBM)


def anywhere():
    return pl.BlockSpec(memory_space=pl.ANY)


def smem():
    return pl.BlockSpec(memory_space=pltpu.SMEM)


SWAP = [(0, 1), (1, 0)]


def sum_over_vert(partial, beside):
    parts = partial.reshape(8, -1, 8, LANES)
    share = jnp.sum(lax.all_to_all(parts, PLANE, 0, 0), axis=0)
    share = jnp.sum(lax.all_to_all(jnp.broadcast_to(share[None], parts.shape), "z", 0, 0), axis=0)
    share, beside = lax.optimization_barrier((share, beside))
    whole = lax.all_to_all(jnp.broadcast_to(share[None], parts.shape), PLANE, 0, 0)
    return whole.reshape(ROW_COUNT, LANES), beside


def f32(*shape):
    return jax.ShapeDtypeStruct(shape, jnp.float32)


def tables_of(kernel, wanted, name, *operands):
    return pl.pallas_call(
        functools.partial(kernel, wanted),
        out_shape=(
            f32(ROWS, LANES), f32(3, VG, ROWS, LANES), f32(6, 5, ROWS, LANES)
        ),
        in_specs=[vmem()] * len(operands),
        out_specs=(vmem(), vmem(), vmem()),
        compiler_params=pltpu.CompilerParams(vmem_limit_bytes=16 * 2**20),
        cost_estimate=pl.CostEstimate(flops=8000000, bytes_accessed=3000000, transcendentals=250000),
        name=name,
    )(*operands)


def body(distribution, collision_rate):
    device = lax.axis_index(VERT)
    place = device.astype(jnp.int32).reshape(1)
    rows = pl.pallas_call(
        send_kernel,
        out_shape=f32(VEL_LOCAL, 2, LANES),
        in_specs=[smem(), hbm()],
        out_specs=vmem(),
        scratch_shapes=[pltpu.VMEM((VEL_LOCAL, 8, LANES), jnp.float32), pltpu.SemaphoreType.DMA],
        compiler_params=pltpu.CompilerParams(vmem_limit_bytes=24 * 2**20),
        cost_estimate=pl.CostEstimate(flops=0, bytes_accessed=600000, transcendentals=0),
        name="send_rows",
    )(place, in_hbm(distribution))
    f_edge = lax.ppermute(rows, "gx", SWAP)
    held = pl.pallas_call(
        hold_kernel,
        out_shape=f32(VEL_LOCAL, ROWS, LANES),
        in_specs=[hbm(), anywhere()],
        out_specs=vmem(),
        scratch_shapes=[pltpu.SemaphoreType.DMA],
        compiler_params=pltpu.CompilerParams(vmem_limit_bytes=16 * 2**20),
        cost_estimate=pl.CostEstimate(flops=0, bytes_accessed=4000000, transcendentals=0),
        name="hold",
    )(in_hbm(distribution), rows)
    f_near = lax.ppermute(distribution, "gy", SWAP)
    kept, kept_edge, groups = pl.pallas_call(
        inside_kernel,
        out_shape=(
            f32(VEL_LOCAL, ROWS, LANES), f32(VEL_LOCAL, 2, LANES), f32(GROUPS, 6, ROWS, LANES)
        ),
        in_specs=[smem(), vmem(), hbm(), hbm()],
        out_specs=(vmem(), vmem(), vmem()),
        scratch_shapes=[
            pltpu.VMEM((VEL_LOCAL, ROWS, LANES), jnp.float32),
            pltpu.VMEM((ROWS, LANES), jnp.float32),
            pltpu.SemaphoreType.DMA((STEPS,)),
            pltpu.SemaphoreType.DMA,
        ],
        compiler_params=pltpu.CompilerParams(vmem_limit_bytes=16 * 2**20),
        cost_estimate=pl.CostEstimate(flops=50000000, bytes_accessed=6000000, transcendentals=0),
        name="move_inside",
    )(place, held, in_hbm(f_near), in_hbm(collision_rate))
    kept_edge = lax.ppermute(kept_edge, "gx", SWAP)
    kept, partial = pl.pallas_call(
        edge_kernel,
        out_shape=(f32(VEL_LOCAL, ROWS, LANES), f32(ROW_COUNT, LANES)),
        in_specs=[smem(), anywhere()] + [vmem()] * 3,
        out_specs=(anywhere(), vmem()),
        scratch_shapes=[
            pltpu.VMEM((GROUPS, 6, ROWS, LANES), jnp.float32),
            pltpu.VMEM((VEL_LOCAL, 8, LANES), jnp.float32),
            pltpu.VMEM((16, LANES), jnp.float32),
            pltpu.VMEM((CHUNK, 48, LANES), jnp.float32),
            pltpu.SemaphoreType.DMA,
        ],
        input_output_aliases={1: 0},
        compiler_params=pltpu.CompilerParams(vmem_limit_bytes=16 * 2**20),
        name="enter_and_sum",
    )(place, kept, groups, f_edge, collision_rate)
    kept_near = lax.ppermute(kept, "gy", SWAP)
    total, kept_edge = sum_over_vert(partial, kept_edge)
    total_near = lax.ppermute(total, "gy", SWAP)
    total_edge = lax.ppermute(total[ROW_PACKED:], "gx", SWAP)
    own = tables_of(table_kernel, "xyz", "tables_own", total, collision_rate)
    near = tables_of(near_kernel, "y", "tables_near", total_near)
    moved_part = pl.pallas_call(
        second_inside_kernel,
        out_shape=f32(VEL_LOCAL, ROWS, LANES),
        in_specs=[smem(), vmem(), hbm()] + [vmem()] * 4,
        out_specs=vmem(),
        scratch_shapes=[
            pltpu.VMEM((VEL_LOCAL, ROWS, LANES), jnp.float32),
            pltpu.SemaphoreType.DMA((STEPS,)),
        ],
        compiler_params=pltpu.CompilerParams(vmem_limit_bytes=16 * 2**20),
        cost_estimate=pl.CostEstimate(flops=50000000, bytes_accessed=6000000, transcendentals=0),
        name="move_inside_two",
    )(place, kept, in_hbm(kept_near), *own[:2], *near[:2])
    return pl.pallas_call(
        second_kernel,
        out_shape=f32(VEL_LOCAL, ROWS, LANES),
        in_specs=[smem()] + [vmem()] * 8,
        out_specs=anywhere(),
        scratch_shapes=[
            pltpu.VMEM((8, LANES), jnp.float32),
            pltpu.VMEM((3, VG, 8, LANES), jnp.float32),
            pltpu.VMEM((2, 5, 8, LANES), jnp.float32),
            pltpu.VMEM((VG + 4, ROWS, LANES), jnp.float32),
            pltpu.VMEM((VEL_LOCAL, ROWS, LANES), jnp.float32),
            pltpu.VMEM((16, LANES), jnp.float32),
            pltpu.VMEM((CHUNK, 48, LANES), jnp.float32),
            pltpu.SemaphoreType.DMA((STEPS,)),
        ],
        compiler_params=pltpu.CompilerParams(vmem_limit_bytes=24 * 2**20),
        name="collide_two",
    )(
        place, moved_part, kept_edge, total, total_near, total_edge, collision_rate, own[2],
        near[2],
    )


def solution(mesh):
    split = Mesh(mesh.devices.reshape(2, 2, 4, 2, 8), ("gx", "gy", "x", "yl", "z"))
    placed = (P(VERT, "gx", "gy"), P("gx", "gy"))
    return jax.shard_map(
        body, mesh=split, in_specs=placed, out_specs=P(VERT, "gx", "gy"), check_vma=False
    )
```
